128 devices in a mesh: rep: 8 (over z_hi, x), fsdp: 16 (over z_lo, y, core).
Axes of the slice: x: 4, y: 4, z: 4 (z_hi: 2, z_lo: 2; z = z_hi * 2 + z_lo), core: 2. Of those that a mesh axis runs over, the one named last changes fastest.
Arguments:
- round_index: int32 [], replicated, may hold values from 0 to 999
- tokens: bfloat16 [8, 8192, 8192], P('rep', 'fsdp'), may hold values from -6 to 6
- cotangent: bfloat16 [8, 8192, 1024], P('rep', 'fsdp'), may hold values from -6 to 6
- params: float32 [8, 8192, 1024], P('rep', 'fsdp'), may hold values from -6 to 6
- momentum: float32 [8, 8192, 1024], P('rep', 'fsdp'), may hold values from -6 to 6
Outputs:
- key_out: bfloat16 [8, 8192, 1024], P('rep', 'fsdp')
- input_grad: bfloat16 [8, 8192, 8192], P('rep', 'fsdp')
- new_params: float32 [8, 8192, 1024], P('rep', 'fsdp')
- new_momentum: float32 [8, 8192, 1024], P('rep', 'fsdp')
The draws below stay inside these ranges and needn't reach their ends.
All inputs are finite; a program needn't handle non-finite values.
Results may differ from the reference program's by a relative error of at most 0.018.
Values may be sent and summed in bfloat16 or wider, within the bound.
No kernel may reach another device: no remote copies, remote signals or barrier semaphores. Data moves between devices by JAX's collectives and lax.ppermute only.
A program may use at most 256 MiB of HBM per device.

```python
import jax
import jax.numpy as jnp
from jax import lax

D = 8192
KV = 1024
TOK_DEV = 512
TOKENS = 8192
N_REPLICAS = 8
N_REP = 8
N_FSDP = 16


def spiked(drawn, own_key, source, target, blocks, factor):
    def block_of(position):
        return (jnp.arange(drawn.shape[position]) // (drawn.shape[position] // blocks)).reshape((-1,) + (1,) * (drawn.ndim - 1 - position))

    near = jax.random.permutation(own_key, blocks)[block_of(target)]
    far = (block_of(target) + blocks // 2) % blocks
    return jnp.where((block_of(source) == near) | (block_of(source) == far), factor * drawn, drawn)


def block_scale(own_key, dims, pieces, low, largest):
    level = 1.0
    for position, blocks in pieces:
        heights = jax.random.uniform(jax.random.fold_in(jax.random.fold_in(own_key, 6), position), (blocks,), jnp.float32, low / len(pieces), largest / len(pieces))
        level = level * jnp.repeat(jnp.exp(heights), dims[position] // blocks).reshape((-1,) + (1,) * (len(dims) - 1 - position))
    return level


def normal_values(stream_key, dims, spread, reach, split=(), held_as=jnp.bfloat16):
    factor_of = block_scale(stream_key, dims, split, -0.22, 0.18) if split else 1.0
    result = jax.random.normal(stream_key, dims, jnp.float32) * spread * factor_of
    return jnp.minimum(jnp.maximum(result, -reach), reach).astype(held_as)


def heavy_noise(stream_key, dims, deviation, most, shards, heavy, kind=jnp.bfloat16):
    entries = deviation * jax.random.normal(stream_key, dims, jnp.float32)
    if shards:
        entries = entries * block_scale(stream_key, dims, shards, -0.22, 0.18)
    return jnp.clip(spiked(entries, jax.random.fold_in(stream_key, 3), *heavy), -most, most).astype(kind)


def setup_inputs(seed: int = 0) -> dict:
    seeds = jax.random.split(jax.random.key(seed), 6)
    return {
        "round_index": jax.random.randint(seeds[0], (), 0, 1000).astype(jnp.int32),
        "tokens": heavy_noise(seeds[1], (N_REPLICAS, TOKENS, D), 1.0, 6.0, ((0, 8), (1, 16)), (1, 2, 16, 2.0)),
        "cotangent": normal_values(seeds[2], (N_REPLICAS, TOKENS, KV), 1.0, 6.0, ((0, 8), (1, 16))),
        "params": normal_values(seeds[3], (N_REPLICAS, D, KV), 1.0, 6.0, ((0, 8), (1, 16)), jnp.float32),
        "momentum": normal_values(seeds[4], (N_REPLICAS, D, KV), 1.0, 6.0, ((0, 8), (1, 16)), jnp.float32),
    }


def replica_work(tokens_one, cotangent_one, params_one, momentum_one):
    scale = D ** -0.5
    weights = params_one.astype(jnp.bfloat16)
    key_out = (jnp.dot(tokens_one, weights, preferred_element_type=jnp.float32) * scale).astype(jnp.bfloat16)
    input_grad = (jnp.dot(cotangent_one, weights.T, preferred_element_type=jnp.float32) * scale).astype(jnp.bfloat16)
    token_blocks = tokens_one.reshape(N_FSDP, TOK_DEV, D)
    cot_blocks = cotangent_one.reshape(N_FSDP, TOK_DEV, KV)

    def accumulate(total, pair):
        partial_value = (jnp.dot(pair[0].T, pair[1], preferred_element_type=jnp.float32) * scale).astype(jnp.bfloat16)
        partial_value = lax.optimization_barrier(partial_value)
        return total + partial_value.astype(jnp.float32), None

    gradient, unused = lax.scan(accumulate, jnp.zeros((D, KV), jnp.float32), (token_blocks, cot_blocks))
    moved = 0.9 * momentum_one + gradient
    stepped = params_one - 0.1 * moved
    return key_out, input_grad, stepped, moved


def reference(round_index, tokens, cotangent, params, momentum):
    key_out, input_grad, stepped, moved = lax.map(lambda items: replica_work(*items), (tokens, cotangent, params, momentum))
    levels = N_REP.bit_length() - 1
    bit = jnp.mod(round_index, levels).astype(jnp.int32)
    partner = jnp.bitwise_xor(jnp.arange(N_REP, dtype=jnp.int32), jnp.left_shift(jnp.int32(1), bit))
    new_params = 0.5 * (stepped + jnp.take(stepped, partner, axis=0))
    new_momentum = 0.5 * (moved + jnp.take(moved, partner, axis=0))
    return key_out, input_grad, new_params, new_momentum
```

```python
import jax
import jax.numpy as jnp
from jax import lax
from jax.experimental import pallas as pl
from jax.experimental.pallas import tpu as pltpu
from jax.sharding import PartitionSpec as P

D = 8192
KV = 1024
ROWS = 512
NZ, NY, NC = 2, 4, 2
SCALE = D ** (-0.5)
LEVELS = 3
TN = (((0,), (0,)), ((), ()))
NT = (((1,), (1,)), ((), ()))
NN = (((1,), (0,)), ((), ()))
F32, BF16 = jnp.float32, jnp.bfloat16

FAR = ((1, 2),)
MIDDLE = ((1, 1), (1, -1), (0, 2))
NEAR = ((0, -1), (0, 1), (1, 0), (0, 0))


def place(z, y, c):
    return (z % NZ) * NY * NC + (y % NY) * NC + c % NC


def shift(dz=0, dy=0, dc=0):
    return [
        (place(z, y, c), place(z + dz, y + dy, c + dc))
        for z in range(NZ)
        for y in range(NY)
        for c in range(NC)
    ]


def y_up(value):
    return lax.ppermute(value, "fsdp", shift(dy=1))


def y_down(value):
    return lax.ppermute(value, "fsdp", shift(dy=-1))


def z_across(value):
    return lax.ppermute(value, "fsdp", shift(dz=1))


def core_swap(value):
    return lax.ppermute(value, "fsdp", shift(dc=1))


def partner_swap(value, level):
    return lax.ppermute(value, "rep", [(r, r ^ (1 << level)) for r in range(1 << LEVELS)])


def columns(offsets, core):
    f = lax.axis_index("fsdp").astype(jnp.int32)
    z, y = f // (NY * NC), (f // NC) % NY
    return jnp.stack([place(z + dz, y + dy, core).astype(jnp.int32) for dz, dy in offsets])


def dot(a, b, dims):
    return lax.dot_general(a, b, dims, preferred_element_type=F32)


def whole(shape):
    return pl.BlockSpec(shape, lambda k, idx: (0,) * len(shape))


def by_column():
    return pl.BlockSpec((ROWS, ROWS), lambda k, idx: (0, idx[k]))


def by_step():
    return pl.BlockSpec((1, ROWS, ROWS), lambda k, idx: (k, 0, 0))


def params_of(flops, nbytes):
    return dict(
        compiler_params=pltpu.CompilerParams(vmem_limit_bytes=36 * 2**20),
        cost_estimate=pl.CostEstimate(flops=flops, bytes_accessed=nbytes, transcendentals=0),
    )


def pack_first(tokens, cot, idx):
    def kernel(idx_ref, tok_ref, cot_ref, out_ref):
        out_ref[:, :KV] = cot_ref[...]
        out_ref[:, KV:] = tok_ref[...]

    return pl.pallas_call(
        kernel,
        grid_spec=pltpu.PrefetchScalarGridSpec(
            num_scalar_prefetch=1,
            grid=(1,),
            in_specs=[by_column(), whole((ROWS, KV))],
            out_specs=whole((ROWS, KV + ROWS)),
        ),
        out_shape=jax.ShapeDtypeStruct((ROWS, KV + ROWS), BF16),
        name="pack_first",
        **params_of(0, 3 * 2**20),
    )(idx, tokens, cot)


def pack(tokens, idx):
    n = idx.shape[0]

    def kernel(idx_ref, tok_ref, out_ref):
        out_ref[0] = tok_ref[...]

    return pl.pallas_call(
        kernel,
        grid_spec=pltpu.PrefetchScalarGridSpec(
            num_scalar_prefetch=1, grid=(n,), in_specs=[by_column()], out_specs=by_step()
        ),
        out_shape=jax.ShapeDtypeStruct((n, ROWS, ROWS), BF16),
        name="pack",
        **params_of(0, n * 2**20),
    )(idx, tokens)


def unpack(target, pieces, idx):
    n = idx.shape[0]

    def kernel(idx_ref, old_ref, piece_ref, out_ref):
        del old_ref
        out_ref[...] = piece_ref[0]

    return pl.pallas_call(
        kernel,
        grid_spec=pltpu.PrefetchScalarGridSpec(
            num_scalar_prefetch=1,
            grid=(n,),
            in_specs=[pl.BlockSpec(memory_space=pl.ANY), by_step()],
            out_specs=by_column(),
        ),
        out_shape=jax.ShapeDtypeStruct(target.shape, BF16),
        input_output_aliases={1: 0},
        name="unpack",
        **params_of(0, n * 2**20),
    )(idx, target, pieces)


def gradients(tokens, other_tokens, cot, first, idx, cuts=None):
    n = idx.shape[0]
    if cuts is None:
        shapes = [(ROWS, KV)] * n
    else:
        shapes = [(hi - lo, KV) for lo, hi in cuts]

    def kernel(idx_ref, tok_ref, oth_ref, cot_ref, cot_oth_ref, *outs):
        step = pl.program_id(0)
        oth = oth_ref[...] if cuts is not None else oth_ref[0]
        total = dot(tok_ref[...], cot_ref[...], TN) + dot(oth, cot_oth_ref[...], TN)
        total = (total * SCALE).astype(BF16)
        if cuts is not None:
            for (lo, hi), out in zip(cuts, outs):
                out[...] = total[lo:hi]
        else:
            for i, out in enumerate(outs):

                @pl.when(step == i)
                def _(out=out):
                    out[...] = total

    if cuts is not None:
        oth_spec = pl.BlockSpec((ROWS, ROWS), lambda k, idx: (0, KV // ROWS))
    else:
        oth_spec = by_step()
    return pl.pallas_call(
        kernel,
        grid_spec=pltpu.PrefetchScalarGridSpec(
            num_scalar_prefetch=1,
            grid=(n,),
            in_specs=[by_column(), oth_spec, whole((ROWS, KV)), whole((ROWS, KV))],
            out_specs=[whole(s) for s in shapes],
        ),
        out_shape=[jax.ShapeDtypeStruct(s, BF16) for s in shapes],
        name="gradients",
        **params_of(n * 4 * ROWS * ROWS * KV, (2 * n + 2) * 2**20),
    )(idx, tokens, other_tokens, cot, first)


def forward(tokens, other_tokens, cot, first, weights, idx, keys=None, grad_in=None):
    n = idx.shape[0]
    last = keys is not None

    def kernel(idx_ref, *refs):
        refs = list(refs)
        tok_ref, oth_ref, cot_ref, cot_oth_ref = refs[:4]
        w_refs = refs[4 : 4 + n]
        rest = refs[4 + n :]
        if last:
            own_in, oth_in, _, own_out, oth_out, gi_ref, back_ref, acc = rest
        else:
            own_out, oth_out, gi_ref, back_ref = rest
            acc = oth_out
        step = pl.program_id(0)

        @pl.when(step == 0)
        def _():
            if last:
                own_out[...] = own_in[...]
                acc[...] = oth_in[...]
            else:
                own_out[...] = jnp.zeros_like(own_out)
                acc[...] = jnp.zeros_like(acc)

        for i, w_ref in enumerate(w_refs):

            @pl.when(step == i)
            def _(w_ref=w_ref):
                own_out[...] += dot(tok_ref[...], w_ref[...], NN)
                acc[...] += dot(oth_ref[0], w_ref[...], NN)
                gi_ref[...] = (dot(cot_ref[...], w_ref[...], NT) * SCALE).astype(BF16)
                back_ref[0] = (dot(cot_oth_ref[...], w_ref[...], NT) * SCALE).astype(BF16)

        if last:

            @pl.when(step == n - 1)
            def _():
                oth_out[...] = (acc[...] * SCALE).astype(BF16)

    in_specs = [by_column(), by_step(), whole((ROWS, KV)), whole((ROWS, KV))]
    in_specs += [whole((ROWS, KV))] * n
    operands = [tokens, other_tokens, cot, first, *weights]
    aliases = {}
    scratch = []
    if last:
        in_specs += [whole((ROWS, KV))] * 2 + [pl.BlockSpec(memory_space=pl.ANY)]
        operands += [*keys, grad_in]
        aliases = {5 + n + 2: 2}
        scratch = [pltpu.VMEM((ROWS, KV), F32)]
    return pl.pallas_call(
        kernel,
        grid_spec=pltpu.PrefetchScalarGridSpec(
            num_scalar_prefetch=1,
            grid=(n,),
            in_specs=in_specs,
            out_specs=[whole((ROWS, KV)), whole((ROWS, KV)), by_column(), by_step()],
            scratch_shapes=scratch,
        ),
        out_shape=[
            jax.ShapeDtypeStruct((ROWS, KV), F32),
            jax.ShapeDtypeStruct((ROWS, KV), BF16 if last else F32),
            jax.ShapeDtypeStruct((ROWS, D), BF16),
            jax.ShapeDtypeStruct((n, ROWS, ROWS), BF16),
        ],
        input_output_aliases=aliases,
        name="forward",
        **params_of(n * 8 * ROWS * ROWS * KV, (3 * n + 8) * 2**20),
    )(idx, *operands)


def one_shard(tokens, cot, weights, keys, grad_in, idx, received=None):
    final = received is not None

    def kernel(idx_ref, tok_ref, cot_ref, w_ref, key_ref, *rest):
        total = key_ref[...] + dot(tok_ref[...], w_ref[...], NN)
        if final:
            rec_ref, _, key_out, gi_ref = rest
            key_out[...] = (total * SCALE + rec_ref[...].astype(F32)).astype(BF16)
        else:
            _, key_out, gi_ref = rest
            key_out[...] = total
        gi_ref[...] = (dot(cot_ref[...], w_ref[...], NT) * SCALE).astype(BF16)

    full = whole((ROWS, KV))
    operands = [tokens, cot, weights, keys] + ([received] if final else []) + [grad_in]
    return pl.pallas_call(
        kernel,
        grid_spec=pltpu.PrefetchScalarGridSpec(
            num_scalar_prefetch=1,
            grid=(1,),
            in_specs=[by_column(), full, full, full]
            + ([full] if final else [])
            + [pl.BlockSpec(memory_space=pl.ANY)],
            out_specs=[full, by_column()],
        ),
        out_shape=[
            jax.ShapeDtypeStruct((ROWS, KV), BF16 if final else F32),
            jax.ShapeDtypeStruct((ROWS, D), BF16),
        ],
        input_output_aliases={len(operands): 1},
        name="one_shard",
        **params_of(4 * ROWS * ROWS * KV, 8 * 2**20),
    )(idx, *operands)


def program_of(level, tokens, cot, params, momentum):
    cuts = ((0, 176), (176, 336), (336, 512))
    (a0, a1), (b0, b1), (c0, c1) = cuts
    core = lax.axis_index("fsdp").astype(jnp.int32) % NC
    far, far_oth = columns(FAR, core), columns(FAR, 1 - core)
    mid, mid_oth = columns(MIDDLE, core), columns(MIDDLE, 1 - core)
    near, near_oth = columns(NEAR, core), columns(NEAR, 1 - core)

    own = params.astype(BF16)
    first = core_swap(pack_first(tokens, cot, far_oth))
    w_0m, w_01, w_10 = y_up(own), y_down(own), z_across(own)
    tok_mid = core_swap(pack(tokens, mid_oth))
    tok_near = core_swap(pack(tokens, near_oth))
    partner_params = partner_swap(own, level)

    t0, t1, t2 = gradients(tokens, first, cot, first, far, cuts)
    t0, t1, t2 = y_up(t0), y_down(t1), z_across(t2)
    p_11, p_1m, p_02 = gradients(tokens, tok_mid, cot, first, mid)
    p_0m, p_01, p_10, p_00 = gradients(tokens, tok_near, cot, first, near)
    p_11 = p_11.at[a0:a1].add(t0)
    p_1m = p_1m.at[b0:b1].add(t1)
    p_02 = p_02.at[c0:c1].add(t2)
    p_11, p_1m, p_02 = y_up(p_11), z_across(p_1m), y_down(p_02)
    p_0m = (p_0m.astype(F32) + p_1m.astype(F32) + p_02.astype(F32)).astype(BF16)
    p_10 = (p_10.astype(F32) + p_11.astype(F32)).astype(BF16)
    p_0m, p_01, p_10 = y_down(p_0m), y_up(p_01), z_across(p_10)
    gradient = (p_00.astype(F32) + p_01.astype(F32)) + (p_0m.astype(F32) + p_10.astype(F32))
    moved = 0.9 * momentum + gradient
    partner_moved = partner_swap(moved.astype(BF16), level).astype(F32)
    new_momentum = 0.5 * (moved + partner_moved)
    partner_stepped = partner_params.astype(F32) - 0.1 * partner_moved
    new_params = 0.5 * ((params - 0.1 * moved) + partner_stepped)

    w_02, w_11, w_1m = y_up(w_0m), y_down(w_10), z_across(w_0m)
    w_12 = jnp.concatenate(
        [y_up(w_1m[a0:a1]), y_down(w_11[b0:b1]), z_across(w_02[c0:c1])], axis=0
    )
    w_12_oth = core_swap(w_12)

    key_own, key_oth, grad_in, back = forward(
        tokens, tok_near, cot, first, (w_0m, w_01, w_10, own), near
    )
    grad_in = unpack(grad_in, core_swap(back), near_oth)
    key_own, key_oth, grad_in, back = forward(
        tokens, tok_mid, cot, first, (w_11, w_1m, w_02), mid, (key_own, key_oth), grad_in
    )
    key_oth = core_swap(key_oth)
    grad_in = unpack(grad_in, core_swap(back), mid_oth)
    key_own, grad_in = one_shard(tokens, cot, w_12, key_own, grad_in, far)
    key_out, grad_in = one_shard(tokens, cot, w_12_oth, key_own, grad_in, far_oth, key_oth)
    return key_out, grad_in, new_params, new_momentum


def body(round_index, tokens, cotangent, params, momentum):
    bit = jnp.mod(round_index, LEVELS)
    branches = [
        lambda *arrays, level=level: program_of(level, *arrays) for level in range(LEVELS)
    ]
    outs = lax.switch(bit, branches, tokens[0], cotangent[0], params[0], momentum[0])
    return tuple(out[None] for out in outs)


def solution(mesh):
    rows = P("rep", "fsdp", None)
    return jax.shard_map(
        body,
        mesh=mesh,
        in_specs=(P(), rows, rows, rows, rows),
        out_specs=(rows, rows, rows, rows),
        check_vma=False,
    )
```

```python
import jax
import jax.numpy as jnp
from jax import lax
from jax.experimental import pallas as pl
from jax.experimental.pallas import tpu as pltpu
from jax.sharding import PartitionSpec as P

D = 8192
KV = 1024
ROWS = 512
NZ, NY, NC = 2, 4, 2
SCALE = D ** (-0.5)
LEVELS = 3
TN = (((0,), (0,)), ((), ()))
NT = (((1,), (1,)), ((), ()))
NN = (((1,), (0,)), ((), ()))
F32, BF16 = jnp.float32, jnp.bfloat16

FAR = ((1, 2),)
MIDDLE = ((1, 1), (1, -1), (0, 2))
NEAR = ((0, -1), (0, 1), (1, 0), (0, 0))


def place(z, y, c):
    return (z % NZ) * NY * NC + (y % NY) * NC + c % NC


def shift(dz=0, dy=0, dc=0):
    return [
        (place(z, y, c), place(z + dz, y + dy, c + dc))
        for z in range(NZ)
        for y in range(NY)
        for c in range(NC)
    ]


def y_up(value):
    return lax.ppermute(value, "fsdp", shift(dy=1))


def y_down(value):
    return lax.ppermute(value, "fsdp", shift(dy=-1))


def z_across(value):
    return lax.ppermute(value, "fsdp", shift(dz=1))


def core_swap(value):
    return lax.ppermute(value, "fsdp", shift(dc=1))


def partner_swap(value, bit):
    def swap(arr, level):
        return lax.ppermute(arr, "rep", [(r, r ^ (1 << level)) for r in range(1 << LEVELS)])

    return lax.switch(bit, [lambda arr, level=level: swap(arr, level) for level in range(LEVELS)], value)


def columns(offsets, core):
    f = lax.axis_index("fsdp").astype(jnp.int32)
    z, y = f // (NY * NC), (f // NC) % NY
    return jnp.stack([place(z + dz, y + dy, core).astype(jnp.int32) for dz, dy in offsets])


def dot(a, b, dims):
    return lax.dot_general(a, b, dims, preferred_element_type=F32)


def whole(shape):
    return pl.BlockSpec(shape, lambda k, idx: (0,) * len(shape))


def by_column():
    return pl.BlockSpec((ROWS, ROWS), lambda k, idx: (0, idx[k]))


def by_step(start=0):
    return pl.BlockSpec((1, ROWS, ROWS), lambda k, idx: (k + start, 0, 0))


def params_of(flops, nbytes, vmem=36):
    flops, nbytes = int(flops), int(nbytes)
    return dict(
        compiler_params=pltpu.CompilerParams(vmem_limit_bytes=vmem * 2**20),
        cost_estimate=pl.CostEstimate(flops=flops, bytes_accessed=nbytes, transcendentals=0),
    )


ANYWHERE = pl.BlockSpec(memory_space=pl.ANY)
IN_HBM = pl.BlockSpec(memory_space=pltpu.HBM)


def slab(idx_ref, k):
    return pl.ds(pl.multiple_of(idx_ref[k] * ROWS, ROWS), ROWS)


def token_slabs(idx_ref, tok_ref, buf, sem, n):
    step = pl.program_id(0)

    def copy(k):
        return pltpu.make_async_copy(tok_ref.at[:, slab(idx_ref, k)], buf.at[k], sem.at[k])

    @pl.when(step == 0)
    def _():
        for k in range(n):
            copy(k).start()

    for k in range(n):

        @pl.when(step == k)
        def _(k=k):
            copy(k).wait()

    return buf[step]


def slab_scratch(n):
    return [pltpu.VMEM((n, ROWS, ROWS), BF16), pltpu.SemaphoreType.DMA((n,))]


def through(in_copies, out_copies):
    for copy in in_copies:
        copy.start()
    for copy, out in zip(in_copies, out_copies):
        copy.wait()
        out.start()
    for out in out_copies:
        out.wait()


def pack_first(tokens, cot, idx, after):
    def kernel(idx_ref, tok_ref, cot_ref, after_ref, out_ref, buf, sem, out_sem):
        del after_ref
        n, rows = 4, ROWS // 4
        ins, outs = [], []
        for i in range(n):
            part = pl.ds(i * rows, rows)
            tok_part, tok_buf = tok_ref.at[part, slab(idx_ref, 0)], buf.at[part, pl.ds(KV, ROWS)]
            ins.append(pltpu.make_async_copy(cot_ref.at[part], buf.at[part, pl.ds(0, KV)], sem.at[i]))
            ins.append(pltpu.make_async_copy(tok_part, tok_buf, sem.at[n + i]))
            outs.append(pltpu.make_async_copy(buf.at[part], out_ref.at[part], out_sem.at[i]))
        for copy in ins:
            copy.start()
        for i in range(n):
            ins[2 * i].wait()
            ins[2 * i + 1].wait()
            outs[i].start()
        for copy in outs:
            copy.wait()

    shape = (ROWS, KV + ROWS)
    return pl.pallas_call(
        kernel,
        grid_spec=pltpu.PrefetchScalarGridSpec(
            num_scalar_prefetch=1,
            grid=(1,),
            in_specs=[IN_HBM, ANYWHERE, ANYWHERE],
            out_specs=ANYWHERE,
            scratch_shapes=[
                pltpu.VMEM(shape, BF16),
                pltpu.SemaphoreType.DMA((8,)),
                pltpu.SemaphoreType.DMA((4,)),
            ],
        ),
        out_shape=jax.ShapeDtypeStruct(shape, BF16),
        name="pack_first",
        **params_of(0, 3 * 2**20, 58),
    )(idx, tokens, cot, after)


def pack(tokens, idx, after):
    n = idx.shape[0]

    def kernel(idx_ref, tok_ref, after_ref, out_ref, buf, sem, out_sem):
        del after_ref
        through(
            [
                pltpu.make_async_copy(tok_ref.at[:, slab(idx_ref, k)], buf.at[k], sem.at[k])
                for k in range(n)
            ],
            [pltpu.make_async_copy(buf.at[k], out_ref.at[k], out_sem.at[k]) for k in range(n)],
        )

    return pl.pallas_call(
        kernel,
        grid_spec=pltpu.PrefetchScalarGridSpec(
            num_scalar_prefetch=1,
            grid=(1,),
            in_specs=[IN_HBM, ANYWHERE],
            out_specs=ANYWHERE,
            scratch_shapes=[
                pltpu.VMEM((n, ROWS, ROWS), BF16),
                pltpu.SemaphoreType.DMA((n,)),
                pltpu.SemaphoreType.DMA((n,)),
            ],
        ),
        out_shape=jax.ShapeDtypeStruct((n, ROWS, ROWS), BF16),
        name="pack",
        **params_of(0, n * 2**20, 58),
    )(idx, tokens, after)


def unpack(target, pieces, idx):
    n = idx.shape[0]

    def kernel(idx_ref, old_ref, piece_ref, out_ref, buf, sem, out_sem):
        del old_ref
        through(
            [pltpu.make_async_copy(piece_ref.at[k], buf.at[k], sem.at[k]) for k in range(n)],
            [
                pltpu.make_async_copy(buf.at[k], out_ref.at[:, slab(idx_ref, k)], out_sem.at[k])
                for k in range(n)
            ],
        )

    return pl.pallas_call(
        kernel,
        grid_spec=pltpu.PrefetchScalarGridSpec(
            num_scalar_prefetch=1,
            grid=(1,),
            in_specs=[ANYWHERE] * 2,
            out_specs=ANYWHERE,
            scratch_shapes=[
                pltpu.VMEM((n, ROWS, ROWS), BF16),
                pltpu.SemaphoreType.DMA((n,)),
                pltpu.SemaphoreType.DMA((n,)),
            ],
        ),
        out_shape=jax.ShapeDtypeStruct(target.shape, BF16),
        input_output_aliases={1: 0},
        name="unpack",
        **params_of(0, n * 2**20),
    )(idx, target, pieces)


def cut_rows(parts):
    n = len(parts)

    def kernel(*refs):
        ins, outs, (buf, sem, out_sem) = refs[:n], refs[n : 2 * n], refs[2 * n :]
        spans = [pl.ds(lo, hi - lo) for _, lo, hi in parts]
        through(
            [
                pltpu.make_async_copy(r.at[d], buf.at[d], sem.at[i])
                for i, (r, d) in enumerate(zip(ins, spans))
            ],
            [
                pltpu.make_async_copy(buf.at[d], r, out_sem.at[i])
                for i, (r, d) in enumerate(zip(outs, spans))
            ],
        )

    return pl.pallas_call(
        kernel,
        in_specs=[ANYWHERE] * n,
        out_specs=[ANYWHERE] * n,
        out_shape=[jax.ShapeDtypeStruct((hi - lo, KV), BF16) for _, lo, hi in parts],
        scratch_shapes=[
            pltpu.VMEM((ROWS, KV), BF16),
            pltpu.SemaphoreType.DMA((n,)),
            pltpu.SemaphoreType.DMA((n,)),
        ],
        name="cut_rows",
        **params_of(0, 2 * 2**20),
    )(*[array for array, _, _ in parts])


def join_rows(pieces, bounds, after):
    n, m = len(pieces), len(after)

    def kernel(*refs):
        ins, out, (buf, sem, out_sem) = refs[:n], refs[n + m], refs[n + m + 1 :]
        spans = [pl.ds(lo, hi - lo) for lo, hi in bounds]
        through(
            [
                pltpu.make_async_copy(r, buf.at[d], sem.at[i])
                for i, (r, d) in enumerate(zip(ins, spans))
            ],
            [
                pltpu.make_async_copy(buf.at[d], out.at[d], out_sem.at[i])
                for i, d in enumerate(spans)
            ],
        )

    return pl.pallas_call(
        kernel,
        in_specs=[ANYWHERE] * (n + m),
        out_specs=ANYWHERE,
        out_shape=jax.ShapeDtypeStruct((ROWS, KV), BF16),
        scratch_shapes=[
            pltpu.VMEM((ROWS, KV), BF16),
            pltpu.SemaphoreType.DMA((n,)),
            pltpu.SemaphoreType.DMA((n,)),
        ],
        name="join_rows",
        **params_of(0, 2 * 2**20),
    )(*pieces, *after)


def held_until(values, after):
    n, m = len(values), len(after)

    def kernel(*refs):
        del refs

    return pl.pallas_call(
        kernel,
        in_specs=[ANYWHERE] * (n + m),
        out_specs=[ANYWHERE] * n,
        out_shape=[jax.ShapeDtypeStruct(v.shape, v.dtype) for v in values],
        input_output_aliases={i: i for i in range(n)},
        name="held_until",
        **params_of(0, 0),
    )(*values, *after)


def gradients(tokens, other_tokens, cot, first, idx, start=0, cuts=None, after=()):
    n = idx.shape[0]
    if cuts is None:
        shapes = [(ROWS, KV)] * n
    else:
        shapes = [(hi - lo, KV) for lo, hi in cuts]

    def kernel(idx_ref, tok_ref, oth_ref, cot_ref, cot_oth_ref, *outs):
        *outs, tok_buf, tok_sem = outs[len(after) :]
        tok = token_slabs(idx_ref, tok_ref, tok_buf, tok_sem, n)
        step = pl.program_id(0)
        oth = oth_ref[...] if cuts is not None else oth_ref[0]
        total = dot(tok, cot_ref[...], TN) + dot(oth, cot_oth_ref[...], TN)
        total = (total * SCALE).astype(BF16)
        if cuts is not None:
            for (lo, hi), out in zip(cuts, outs):
                out[...] = total[lo:hi]
        else:
            for i, out in enumerate(outs):

                @pl.when(step == i)
                def _(out=out):
                    out[...] = total

    if cuts is not None:
        oth_spec = pl.BlockSpec((ROWS, ROWS), lambda k, idx: (0, KV // ROWS))
    else:
        oth_spec = by_step(start)
    return pl.pallas_call(
        kernel,
        grid_spec=pltpu.PrefetchScalarGridSpec(
            num_scalar_prefetch=1,
            grid=(n,),
            in_specs=[IN_HBM, oth_spec, whole((ROWS, KV)), whole((ROWS, KV))]
            + [ANYWHERE] * len(after),
            out_specs=[whole(s) for s in shapes],
            scratch_shapes=slab_scratch(n),
        ),
        out_shape=[jax.ShapeDtypeStruct(s, BF16) for s in shapes],
        name="gradients",
        **params_of(n * 4 * ROWS * ROWS * KV, (2 * n + 2) * 2**20, 58 if n == 1 else 36),
    )(idx, tokens, other_tokens, cot, first, *after)


def forward(tokens, other_tokens, cot, first, weights, idx, start, after, keys=None, grad_in=None):
    n, m = idx.shape[0], len(after)
    last = keys is not None

    def kernel(idx_ref, tok_ref, oth_ref, cot_ref, cot_oth_ref, *refs):
        w_refs, rest = refs[:n], refs[n + m :]
        if last:
            own_in, oth_in, _, own_out, oth_out, gi_ref, back_ref, *rest, acc = rest
        else:
            own_out, oth_out, gi_ref, back_ref, *rest = rest
            acc = oth_out
        w_buf, sem, tok_buf, tok_sem = rest
        step = pl.program_id(0)

        @pl.when(step == 0)
        def _():
            for i, w_ref in enumerate(w_refs):
                pltpu.make_async_copy(w_ref, w_buf.at[i], sem.at[i]).start()
            if last:
                own_out[...] = own_in[...]
                acc[...] = oth_in[...]
            else:
                own_out[...] = jnp.zeros_like(own_out)
                acc[...] = jnp.zeros_like(acc)

        for i, w_ref in enumerate(w_refs):

            @pl.when(step == i)
            def _(i=i, w_ref=w_ref):
                pltpu.make_async_copy(w_ref, w_buf.at[i], sem.at[i]).wait()

        w = w_buf[step]
        tok = token_slabs(idx_ref, tok_ref, tok_buf, tok_sem, n)
        own_out[...] += dot(tok, w, NN)
        acc[...] += dot(oth_ref[0], w, NN)
        gi_ref[...] = (dot(cot_ref[...], w, NT) * SCALE).astype(BF16)
        back_ref[0] = (dot(cot_oth_ref[...], w, NT) * SCALE).astype(BF16)

        if last:

            @pl.when(step == n - 1)
            def _():
                oth_out[...] = (acc[...] * SCALE).astype(BF16)

    in_specs = [IN_HBM, by_step(start), whole((ROWS, KV)), whole((ROWS, KV))]
    in_specs += [ANYWHERE] * (n + m)
    operands = [tokens, other_tokens, cot, first, *weights, *after]
    aliases = {}
    scratch = [pltpu.VMEM((n, ROWS, KV), BF16), pltpu.SemaphoreType.DMA((n,)), *slab_scratch(n)]
    if last:
        in_specs += [whole((ROWS, KV))] * 2 + [ANYWHERE]
        operands += [*keys, grad_in]
        aliases = {len(operands): 2}
        scratch += [pltpu.VMEM((ROWS, KV), F32)]
    return pl.pallas_call(
        kernel,
        grid_spec=pltpu.PrefetchScalarGridSpec(
            num_scalar_prefetch=1,
            grid=(n,),
            in_specs=in_specs,
            out_specs=[whole((ROWS, KV)), whole((ROWS, KV)), by_column(), by_step()],
            scratch_shapes=scratch,
        ),
        out_shape=[
            jax.ShapeDtypeStruct((ROWS, KV), F32),
            jax.ShapeDtypeStruct((ROWS, KV), BF16 if last else F32),
            jax.ShapeDtypeStruct((ROWS, D), BF16),
            jax.ShapeDtypeStruct((n, ROWS, ROWS), BF16),
        ],
        input_output_aliases=aliases,
        name="forward",
        **params_of(n * 8 * ROWS * ROWS * KV, (3 * n + 8) * 2**20),
    )(idx, *operands)


def one_shard(tokens, cot, weights, keys, grad_in, idx, received=None):
    final = received is not None
    tile = ROWS // 2

    def kernel(idx_ref, tok_ref, cot_ref, w_ref, key_ref, *rest):
        *rest, tok_buf, sem = rest
        step, n = pl.program_id(0), ROWS // tile
        part = [pl.ds(i * tile, tile) for i in range(n)]
        copies = [
            pltpu.make_async_copy(tok_ref.at[p, slab(idx_ref, 0)], tok_buf.at[p], sem.at[i])
            for i, p in enumerate(part)
        ]

        @pl.when(step == 0)
        def _():
            for copy in copies:
                copy.start()

        for i, copy in enumerate(copies):

            @pl.when(step == i)
            def _(copy=copy):
                copy.wait()

        tok = tok_buf[pl.ds(pl.multiple_of(step * tile, tile), tile)]
        total = key_ref[...] + dot(tok, w_ref[...], NN)
        if final:
            rec_ref, _, key_out, gi_ref = rest
            key_out[...] = (total * SCALE + rec_ref[...].astype(F32)).astype(BF16)
        else:
            _, key_out, gi_ref = rest
            key_out[...] = total
        gi_ref[...] = (dot(cot_ref[...], w_ref[...], NT) * SCALE).astype(BF16)

    def wide():
        return pl.BlockSpec((tile, KV), lambda k, idx: (k, 0))

    def narrow():
        return pl.BlockSpec((tile, ROWS), lambda k, idx: (k, idx[0]))

    operands = [tokens, cot, weights, keys] + ([received] if final else []) + [grad_in]
    return pl.pallas_call(
        kernel,
        grid_spec=pltpu.PrefetchScalarGridSpec(
            num_scalar_prefetch=1,
            grid=(ROWS // tile,),
            in_specs=[IN_HBM, wide(), whole((ROWS, KV)), wide()]
            + ([wide()] if final else [])
            + [ANYWHERE],
            out_specs=[wide(), narrow()],
            scratch_shapes=[
                pltpu.VMEM((ROWS, ROWS), BF16),
                pltpu.SemaphoreType.DMA((ROWS // tile,)),
            ],
        ),
        out_shape=[
            jax.ShapeDtypeStruct((ROWS, KV), BF16 if final else F32),
            jax.ShapeDtypeStruct((ROWS, D), BF16),
        ],
        input_output_aliases={len(operands): 1},
        name="one_shard",
        **params_of(4 * ROWS * ROWS * KV, 8 * 2**20),
    )(idx, *operands)


def body(round_index, tokens, cotangent, params, momentum):
    tokens, cot, params, momentum = tokens[0], cotangent[0], params[0], momentum[0]
    bit = jnp.mod(round_index, LEVELS)
    half, cut, end = ROWS // 2, 176, 336
    core = lax.axis_index("fsdp").astype(jnp.int32) % NC
    far, far_oth = columns(FAR, core), columns(FAR, 1 - core)
    mid, mid_oth = columns(MIDDLE, core), columns(MIDDLE, 1 - core)
    near, near_oth = columns(NEAR, core), columns(NEAR, 1 - core)
    rest, rest_oth = columns(MIDDLE + NEAR, core), columns(MIDDLE + NEAR, 1 - core)

    own = params.astype(BF16)
    w_0m, w_01, w_10 = y_up(own), y_down(own), z_across(own)

    packed = pack_first(tokens, cot, far_oth, own)
    first = core_swap(packed)
    others = core_swap(pack(tokens, rest_oth, packed))

    t0, t1 = gradients(tokens, first, cot, first, far, cuts=((0, half), (half, ROWS)))
    (t1,) = held_until((t1,), (others,))
    t0, t1 = y_up(t0), y_down(t1)
    p_11, p_1m, p_02, p_0m, p_01, p_10, p_00 = gradients(
        tokens, others, cot, first, rest
    )
    p_11 = p_11.at[:half].add(t0)
    p_1m = p_1m.at[half:].add(t1)
    p_11, p_1m, p_02 = held_until((p_11, p_1m, p_02), (w_0m, w_01, w_10))
    key_own, key_oth, grad_in, back = forward(
        tokens, others, cot, first, (w_0m, w_01, w_10, own), near, len(MIDDLE), (p_11, p_1m, p_02)
    )
    p_11, p_1m, p_02 = y_up(p_11), z_across(p_1m), y_down(p_02)
    p_0m = (p_0m.astype(F32) + p_1m.astype(F32) + p_02.astype(F32)).astype(BF16)
    p_10 = (p_10.astype(F32) + p_11.astype(F32)).astype(BF16)
    p_01, own = held_until((p_01, own), (key_own, p_0m, p_10))
    p_0m, p_01, p_10 = y_down(p_0m), y_up(p_01), z_across(p_10)
    partner_params = partner_swap(own, bit)
    gradient = (p_00.astype(F32) + p_01.astype(F32)) + (p_0m.astype(F32) + p_10.astype(F32))
    moved = 0.9 * momentum + gradient

    grad_in = unpack(grad_in, core_swap(back), near_oth)
    w_0m, w_10 = held_until((w_0m, w_10), (p_0m, p_01, p_10, partner_params))
    w_02, w_11, w_1m = y_up(w_0m), y_down(w_10), z_across(w_0m)
    partner_moved = partner_swap(moved.astype(BF16), bit)
    bounds = (0, cut), (cut, end), (end, ROWS)
    pieces = [w[lo:hi] for w, (lo, hi) in zip((w_1m, w_11, w_02), bounds)]
    thirds = y_up(pieces[0]), y_down(pieces[1]), z_across(pieces[2])
    theirs = partner_moved.astype(F32)
    new_momentum = 0.5 * (moved + theirs)
    partner_stepped = partner_params.astype(F32) - 0.1 * theirs
    new_params = 0.5 * ((params - 0.1 * moved) + partner_stepped)
    key_own, key_oth, grad_in, back = forward(
        tokens,
        others,
        cot,
        first,
        (w_11, w_1m, w_02),
        mid,
        0,
        (partner_moved, *pieces),
        (key_own, key_oth),
        grad_in,
    )
    key_oth = core_swap(key_oth)
    (w_12,) = held_until((jnp.concatenate(thirds, axis=0),), (new_params, new_momentum))
    w_12_oth = core_swap(w_12)
    grad_in = unpack(grad_in, core_swap(back), mid_oth)
    key_own, grad_in = one_shard(tokens, cot, w_12, key_own, grad_in, far)
    key_out, grad_in = one_shard(tokens, cot, w_12_oth, key_own, grad_in, far_oth, key_oth)
    return key_out[None], grad_in[None], new_params[None], new_momentum[None]


def solution(mesh):
    rows = P("rep", "fsdp", None)
    return jax.shard_map(
        body,
        mesh=mesh,
        in_specs=(P(), rows, rows, rows, rows),
        out_specs=(rows, rows, rows, rows),
        check_vma=False,
    )
```

```python
import jax
import jax.numpy as jnp
from jax import lax
from jax.experimental import pallas as pl
from jax.experimental.pallas import tpu as pltpu
from jax.sharding import PartitionSpec as P

D = 8192
KV = 1024
ROWS = 512
NZ, NY, NC = 2, 4, 2
SCALE = D ** (-0.5)
LEVELS = 3
TN = (((0,), (0,)), ((), ()))
NT = (((1,), (1,)), ((), ()))
NN = (((1,), (0,)), ((), ()))
F32, BF16 = jnp.float32, jnp.bfloat16

FAR = ((1, 2),)
MIDDLE = ((1, 1), (1, -1), (0, 2))
NEAR = ((0, -1), (0, 1), (1, 0), (0, 0))


def place(z, y, c):
    return (z % NZ) * NY * NC + (y % NY) * NC + c % NC


def shift(dz=0, dy=0, dc=0):
    return [
        (place(z, y, c), place(z + dz, y + dy, c + dc))
        for z in range(NZ)
        for y in range(NY)
        for c in range(NC)
    ]


def y_up(value):
    return lax.ppermute(value, "fsdp", shift(dy=1))


def y_down(value):
    return lax.ppermute(value, "fsdp", shift(dy=-1))


def z_across(value):
    return lax.ppermute(value, "fsdp", shift(dz=1))


def core_swap(value):
    return lax.ppermute(value, "fsdp", shift(dc=1))


def partner_swap(value, bit):
    def swap(arr, level):
        return lax.ppermute(arr, "rep", [(r, r ^ (1 << level)) for r in range(1 << LEVELS)])

    return lax.switch(bit, [lambda arr, level=level: swap(arr, level) for level in range(LEVELS)], value)


def columns(offsets, core):
    f = lax.axis_index("fsdp").astype(jnp.int32)
    z, y = f // (NY * NC), (f // NC) % NY
    return jnp.stack([place(z + dz, y + dy, core).astype(jnp.int32) for dz, dy in offsets])


def dot(a, b, dims):
    return lax.dot_general(a, b, dims, preferred_element_type=F32)


def whole(shape):
    return pl.BlockSpec(shape, lambda k, idx: (0,) * len(shape))


def by_column():
    return pl.BlockSpec((ROWS, ROWS), lambda k, idx: (0, idx[k]))


def by_step():
    return pl.BlockSpec((1, ROWS, ROWS), lambda k, idx: (k, 0, 0))


def params_of(flops, nbytes, vmem=36):
    flops, nbytes = int(flops), int(nbytes)
    return dict(
        compiler_params=pltpu.CompilerParams(vmem_limit_bytes=vmem * 2**20),
        cost_estimate=pl.CostEstimate(flops=flops, bytes_accessed=nbytes, transcendentals=0),
    )


ANYWHERE = pl.BlockSpec(memory_space=pl.ANY)
IN_HBM = pl.BlockSpec(memory_space=pltpu.HBM)


def slab(idx_ref, k):
    return pl.ds(pl.multiple_of(idx_ref[k] * ROWS, ROWS), ROWS)


def token_slabs(idx_ref, tok_ref, buf, sem, n):
    step = pl.program_id(0)

    def copy(k):
        return pltpu.make_async_copy(tok_ref.at[:, slab(idx_ref, k)], buf.at[k], sem.at[k])

    @pl.when(step == 0)
    def _():
        for k in range(n):
            copy(k).start()

    for k in range(n):

        @pl.when(step == k)
        def _(k=k):
            copy(k).wait()

    return buf[step]


def slab_scratch(n):
    return [pltpu.VMEM((n, ROWS, ROWS), BF16), pltpu.SemaphoreType.DMA((n,))]


def through(in_copies, out_copies):
    for copy in in_copies:
        copy.start()
    for copy, out in zip(in_copies, out_copies):
        copy.wait()
        out.start()
    for out in out_copies:
        out.wait()


def pack_first(tokens, cot, idx, after):
    def kernel(idx_ref, tok_ref, cot_ref, after_ref, out_ref, buf, sem, out_sem):
        del after_ref
        n, rows = 4, ROWS // 4
        ins, outs = [], []
        for i in range(n):
            part = pl.ds(i * rows, rows)
            tok_part, tok_buf = tok_ref.at[part, slab(idx_ref, 0)], buf.at[part, pl.ds(KV, ROWS)]
            ins.append(pltpu.make_async_copy(cot_ref.at[part], buf.at[part, pl.ds(0, KV)], sem.at[i]))
            ins.append(pltpu.make_async_copy(tok_part, tok_buf, sem.at[n + i]))
            outs.append(pltpu.make_async_copy(buf.at[part], out_ref.at[part], out_sem.at[i]))
        for copy in ins:
            copy.start()
        for i in range(n):
            ins[2 * i].wait()
            ins[2 * i + 1].wait()
            outs[i].start()
        for copy in outs:
            copy.wait()

    shape = (ROWS, KV + ROWS)
    return pl.pallas_call(
        kernel,
        grid_spec=pltpu.PrefetchScalarGridSpec(
            num_scalar_prefetch=1,
            grid=(1,),
            in_specs=[IN_HBM, ANYWHERE, ANYWHERE],
            out_specs=ANYWHERE,
            scratch_shapes=[
                pltpu.VMEM(shape, BF16),
                pltpu.SemaphoreType.DMA((8,)),
                pltpu.SemaphoreType.DMA((4,)),
            ],
        ),
        out_shape=jax.ShapeDtypeStruct(shape, BF16),
        name="pack_first",
        **params_of(0, 3 * 2**20, 58),
    )(idx, tokens, cot, after)


def unpack(target, pieces, idx):
    n = idx.shape[0]

    def kernel(idx_ref, old_ref, piece_ref, out_ref, buf, sem, out_sem):
        del old_ref
        through(
            [pltpu.make_async_copy(piece_ref.at[k], buf.at[k], sem.at[k]) for k in range(n)],
            [
                pltpu.make_async_copy(buf.at[k], out_ref.at[:, slab(idx_ref, k)], out_sem.at[k])
                for k in range(n)
            ],
        )

    return pl.pallas_call(
        kernel,
        grid_spec=pltpu.PrefetchScalarGridSpec(
            num_scalar_prefetch=1,
            grid=(1,),
            in_specs=[ANYWHERE] * 2,
            out_specs=ANYWHERE,
            scratch_shapes=[
                pltpu.VMEM((n, ROWS, ROWS), BF16),
                pltpu.SemaphoreType.DMA((n,)),
                pltpu.SemaphoreType.DMA((n,)),
            ],
        ),
        out_shape=jax.ShapeDtypeStruct(target.shape, BF16),
        input_output_aliases={1: 0},
        name="unpack",
        **params_of(0, n * 2**20),
    )(idx, target, pieces)


def held_until(values, after):
    n, m = len(values), len(after)

    def kernel(*refs):
        del refs

    return pl.pallas_call(
        kernel,
        in_specs=[ANYWHERE] * (n + m),
        out_specs=[ANYWHERE] * n,
        out_shape=[jax.ShapeDtypeStruct(v.shape, v.dtype) for v in values],
        input_output_aliases={i: i for i in range(n)},
        name="held_until",
        **params_of(0, 0),
    )(*values, *after)


def gradients(tokens, other_tokens, cot, first, idx, cuts=None, after=()):
    n = idx.shape[0]
    if cuts is None:
        shapes = [(ROWS, KV)] * n
    else:
        shapes = [(hi - lo, KV) for lo, hi in cuts]

    def kernel(idx_ref, tok_ref, oth_ref, cot_ref, cot_oth_ref, *outs):
        outs = outs[len(after) :]
        outs, scratch = outs[: len(shapes)], outs[len(shapes) :]
        tok = token_slabs(idx_ref, tok_ref, *scratch[:2], n)
        step = pl.program_id(0)
        oth = oth_ref[...] if cuts is not None else token_slabs(idx_ref, oth_ref, *scratch[2:], n)
        total = dot(tok, cot_ref[...], TN) + dot(oth, cot_oth_ref[...], TN)
        total = (total * SCALE).astype(BF16)
        if cuts is not None:
            for (lo, hi), out in zip(cuts, outs):
                out[...] = total[lo:hi]
        else:
            for i, out in enumerate(outs):

                @pl.when(step == i)
                def _(out=out):
                    out[...] = total

    if cuts is not None:
        oth_spec = pl.BlockSpec((ROWS, ROWS), lambda k, idx: (0, KV // ROWS))
    else:
        oth_spec = IN_HBM
    return pl.pallas_call(
        kernel,
        grid_spec=pltpu.PrefetchScalarGridSpec(
            num_scalar_prefetch=1,
            grid=(n,),
            in_specs=[IN_HBM, oth_spec, whole((ROWS, KV)), whole((ROWS, KV))]
            + [ANYWHERE] * len(after),
            out_specs=[whole(s) for s in shapes],
            scratch_shapes=slab_scratch(n) * (1 if cuts is not None else 2),
        ),
        out_shape=[jax.ShapeDtypeStruct(s, BF16) for s in shapes],
        name="gradients",
        **params_of(n * 4 * ROWS * ROWS * KV, (2 * n + 2) * 2**20, 58 if n == 1 else 36),
    )(idx, tokens, other_tokens, cot, first, *after)


def forward(tokens, other_tokens, cot, first, weights, idx, after, keys=None, grad_in=None):
    n, m = idx.shape[0], len(after)
    last = keys is not None

    def kernel(idx_ref, tok_ref, oth_ref, cot_ref, cot_oth_ref, *refs):
        w_refs, rest = refs[:n], refs[n + m :]
        if last:
            own_in, oth_in, _, own_out, oth_out, gi_ref, back_ref, *rest, acc = rest
        else:
            own_out, oth_out, gi_ref, back_ref, *rest = rest
            acc = oth_out
        w_buf, sem, *slabs = rest
        step = pl.program_id(0)

        @pl.when(step == 0)
        def _():
            for i, w_ref in enumerate(w_refs):
                pltpu.make_async_copy(w_ref, w_buf.at[i], sem.at[i]).start()
            if last:
                own_out[...] = own_in[...]
                acc[...] = oth_in[...]
            else:
                own_out[...] = jnp.zeros_like(own_out)
                acc[...] = jnp.zeros_like(acc)

        for i, w_ref in enumerate(w_refs):

            @pl.when(step == i)
            def _(i=i, w_ref=w_ref):
                pltpu.make_async_copy(w_ref, w_buf.at[i], sem.at[i]).wait()

        w = w_buf[step]
        tok = token_slabs(idx_ref, tok_ref, *slabs[:2], n)
        oth = token_slabs(idx_ref, oth_ref, *slabs[2:], n)
        own_out[...] += dot(tok, w, NN)
        acc[...] += dot(oth, w, NN)
        gi_ref[...] = (dot(cot_ref[...], w, NT) * SCALE).astype(BF16)
        back_ref[0] = (dot(cot_oth_ref[...], w, NT) * SCALE).astype(BF16)

        if last:

            @pl.when(step == n - 1)
            def _():
                oth_out[...] = (acc[...] * SCALE).astype(BF16)

    in_specs = [IN_HBM, IN_HBM, whole((ROWS, KV)), whole((ROWS, KV))]
    in_specs += [ANYWHERE] * (n + m)
    operands = [tokens, other_tokens, cot, first, *weights, *after]
    aliases = {}
    scratch = [pltpu.VMEM((n, ROWS, KV), BF16), pltpu.SemaphoreType.DMA((n,)), *slab_scratch(n) * 2]
    if last:
        in_specs += [whole((ROWS, KV))] * 2 + [ANYWHERE]
        operands += [*keys, grad_in]
        aliases = {len(operands): 2}
        scratch += [pltpu.VMEM((ROWS, KV), F32)]
    return pl.pallas_call(
        kernel,
        grid_spec=pltpu.PrefetchScalarGridSpec(
            num_scalar_prefetch=1,
            grid=(n,),
            in_specs=in_specs,
            out_specs=[whole((ROWS, KV)), whole((ROWS, KV)), by_column(), by_step()],
            scratch_shapes=scratch,
        ),
        out_shape=[
            jax.ShapeDtypeStruct((ROWS, KV), F32),
            jax.ShapeDtypeStruct((ROWS, KV), BF16 if last else F32),
            jax.ShapeDtypeStruct((ROWS, D), BF16),
            jax.ShapeDtypeStruct((n, ROWS, ROWS), BF16),
        ],
        input_output_aliases=aliases,
        name="forward",
        **params_of(n * 8 * ROWS * ROWS * KV, (3 * n + 8) * 2**20),
    )(idx, *operands)


def one_shard(tokens, cot, weights, keys, grad_in, idx, received=None):
    final = received is not None
    tile = ROWS // 2

    def kernel(idx_ref, tok_ref, cot_ref, w_ref, key_ref, *rest):
        *rest, tok_buf, sem = rest
        step, n = pl.program_id(0), ROWS // tile
        part = [pl.ds(i * tile, tile) for i in range(n)]
        copies = [
            pltpu.make_async_copy(tok_ref.at[p, slab(idx_ref, 0)], tok_buf.at[p], sem.at[i])
            for i, p in enumerate(part)
        ]

        @pl.when(step == 0)
        def _():
            for copy in copies:
                copy.start()

        for i, copy in enumerate(copies):

            @pl.when(step == i)
            def _(copy=copy):
                copy.wait()

        tok = tok_buf[pl.ds(pl.multiple_of(step * tile, tile), tile)]
        total = key_ref[...] + dot(tok, w_ref[...], NN)
        if final:
            rec_ref, _, key_out, gi_ref = rest
            key_out[...] = (total * SCALE + rec_ref[...].astype(F32)).astype(BF16)
        else:
            _, key_out, gi_ref = rest
            key_out[...] = total
        gi_ref[...] = (dot(cot_ref[...], w_ref[...], NT) * SCALE).astype(BF16)

    def wide():
        return pl.BlockSpec((tile, KV), lambda k, idx: (k, 0))

    def narrow():
        return pl.BlockSpec((tile, ROWS), lambda k, idx: (k, idx[0]))

    operands = [tokens, cot, weights, keys] + ([received] if final else []) + [grad_in]
    return pl.pallas_call(
        kernel,
        grid_spec=pltpu.PrefetchScalarGridSpec(
            num_scalar_prefetch=1,
            grid=(ROWS // tile,),
            in_specs=[IN_HBM, wide(), whole((ROWS, KV)), wide()]
            + ([wide()] if final else [])
            + [ANYWHERE],
            out_specs=[wide(), narrow()],
            scratch_shapes=[
                pltpu.VMEM((ROWS, ROWS), BF16),
                pltpu.SemaphoreType.DMA((ROWS // tile,)),
            ],
        ),
        out_shape=[
            jax.ShapeDtypeStruct((ROWS, KV), BF16 if final else F32),
            jax.ShapeDtypeStruct((ROWS, D), BF16),
        ],
        input_output_aliases={len(operands): 1},
        name="one_shard",
        **params_of(4 * ROWS * ROWS * KV, 8 * 2**20),
    )(idx, *operands)


def body(round_index, tokens, cotangent, params, momentum):
    tokens, cot, params, momentum = tokens[0], cotangent[0], params[0], momentum[0]
    bit = jnp.mod(round_index, LEVELS)
    half = ROWS // 2
    core = lax.axis_index("fsdp").astype(jnp.int32) % NC
    far, far_oth = columns(FAR, core), columns(FAR, 1 - core)
    mid, mid_oth = columns(MIDDLE, core), columns(MIDDLE, 1 - core)
    near, near_oth = columns(NEAR, core), columns(NEAR, 1 - core)
    rest = columns(MIDDLE + NEAR, core)

    own = params.astype(BF16)
    w_0m, w_01, w_10 = y_up(own), y_down(own), z_across(own)

    packed = pack_first(tokens, cot, far_oth, own)
    first = core_swap(packed)
    others = core_swap(tokens)

    t0, t1 = gradients(tokens, first, cot, first, far, cuts=((0, half), (half, ROWS)))
    (t1,) = held_until((t1,), (others,))
    t0, t1 = y_up(t0), y_down(t1)
    p_11, p_1m, p_02, p_0m, p_01, p_10, p_00 = gradients(
        tokens, others, cot, first, rest
    )
    p_11 = p_11.at[:half].add(t0)
    p_1m = p_1m.at[half:].add(t1)
    p_11, p_1m, p_02 = held_until((p_11, p_1m, p_02), (w_0m, w_01, w_10))
    key_own, key_oth, grad_in, back = forward(
        tokens, others, cot, first, (w_0m, w_01, w_10, own), near, (p_11, p_1m, p_02)
    )
    p_11, p_1m, p_02 = y_up(p_11), z_across(p_1m), y_down(p_02)
    p_0m = (p_0m.astype(F32) + p_1m.astype(F32) + p_02.astype(F32)).astype(BF16)
    p_10 = (p_10.astype(F32) + p_11.astype(F32)).astype(BF16)
    p_01, own = held_until((p_01, own), (key_own, p_0m, p_10))
    p_0m, p_01, p_10 = y_down(p_0m), y_up(p_01), z_across(p_10)
    partner_params = partner_swap(own, bit)
    gradient = (p_00.astype(F32) + p_01.astype(F32)) + (p_0m.astype(F32) + p_10.astype(F32))
    moved = 0.9 * momentum + gradient

    grad_in = unpack(grad_in, core_swap(back), near_oth)
    w_0m, w_10 = held_until((w_0m, w_10), (p_0m, p_01, p_10, partner_params))
    w_02, w_11, w_1m = y_up(w_0m), y_down(w_10), z_across(w_0m)
    (moved_sent,) = held_until((moved.astype(BF16),), (grad_in,))
    partner_moved = partner_swap(moved_sent, bit)
    pieces = w_1m[:half], w_11[half:]
    halves = y_up(pieces[0]), y_down(pieces[1])
    theirs = partner_moved.astype(F32)
    new_momentum = 0.5 * (moved + theirs)
    partner_stepped = partner_params.astype(F32) - 0.1 * theirs
    new_params = 0.5 * ((params - 0.1 * moved) + partner_stepped)
    key_own, key_oth, grad_in, back = forward(
        tokens,
        others,
        cot,
        first,
        (w_11, w_1m, w_02),
        mid,
        (partner_moved, *pieces),
        (key_own, key_oth),
        grad_in,
    )
    key_oth = core_swap(key_oth)
    (w_12,) = held_until((jnp.concatenate(halves, axis=0),), (new_params, new_momentum))
    w_12_oth = core_swap(w_12)
    grad_in = unpack(grad_in, core_swap(back), mid_oth)
    key_own, grad_in = one_shard(tokens, cot, w_12, key_own, grad_in, far)
    key_out, grad_in = one_shard(tokens, cot, w_12_oth, key_own, grad_in, far_oth, key_oth)
    return key_out[None], grad_in[None], new_params[None], new_momentum[None]


def solution(mesh):
    rows = P("rep", "fsdp", None)
    return jax.shard_map(
        body,
        mesh=mesh,
        in_specs=(P(), rows, rows, rows, rows),
        out_specs=(rows, rows, rows, rows),
        check_vma=False,
    )
```

```python
import jax
import jax.numpy as jnp
from jax import lax
from jax.experimental import pallas as pl
from jax.experimental.pallas import tpu as pltpu
from jax.sharding import PartitionSpec as P

D = 8192
KV = 1024
ROWS = 512
NZ, NY, NC = 2, 4, 2
SCALE = D ** (-0.5)
LEVELS = 3
TN = (((0,), (0,)), ((), ()))
NT = (((1,), (1,)), ((), ()))
NN = (((1,), (0,)), ((), ()))
F32, BF16 = jnp.float32, jnp.bfloat16

FAR = ((1, 2),)
MIDDLE = ((1, 1), (1, -1), (0, 2))
NEAR = ((0, -1), (0, 1), (1, 0), (0, 0))


def place(z, y, c):
    return (z % NZ) * NY * NC + (y % NY) * NC + c % NC


def shift(dz=0, dy=0, dc=0):
    return [
        (place(z, y, c), place(z + dz, y + dy, c + dc))
        for z in range(NZ)
        for y in range(NY)
        for c in range(NC)
    ]


def y_up(value):
    return lax.ppermute(value, "fsdp", shift(dy=1))


def y_down(value):
    return lax.ppermute(value, "fsdp", shift(dy=-1))


def z_across(value):
    return lax.ppermute(value, "fsdp", shift(dz=1))


def core_swap(value):
    return lax.ppermute(value, "fsdp", shift(dc=1))


def partner_swap(value, bit):
    def swap(arr, level):
        return lax.ppermute(arr, "rep", [(r, r ^ (1 << level)) for r in range(1 << LEVELS)])

    return lax.switch(bit, [lambda arr, level=level: swap(arr, level) for level in range(LEVELS)], value)


def columns(offsets, core):
    f = lax.axis_index("fsdp").astype(jnp.int32)
    z, y = f // (NY * NC), (f // NC) % NY
    return jnp.stack([place(z + dz, y + dy, core).astype(jnp.int32) for dz, dy in offsets])


def dot(a, b, dims):
    return lax.dot_general(a, b, dims, preferred_element_type=F32)


def whole(shape):
    return pl.BlockSpec(shape, lambda k, idx: (0,) * len(shape))


def by_column():
    return pl.BlockSpec((ROWS, ROWS), lambda k, idx: (0, idx[k]))


def by_step():
    return pl.BlockSpec((1, ROWS, ROWS), lambda k, idx: (k, 0, 0))


def params_of(flops, nbytes, vmem=36):
    flops, nbytes = int(flops), int(nbytes)
    return dict(
        compiler_params=pltpu.CompilerParams(vmem_limit_bytes=vmem * 2**20),
        cost_estimate=pl.CostEstimate(flops=flops, bytes_accessed=nbytes, transcendentals=0),
    )


ANYWHERE = pl.BlockSpec(memory_space=pl.ANY)
IN_HBM = pl.BlockSpec(memory_space=pltpu.HBM)


def slab(idx_ref, k):
    return pl.ds(pl.multiple_of(idx_ref[k] * ROWS, ROWS), ROWS)


def token_slabs(idx_ref, tok_ref, buf, sem, n):
    step = pl.program_id(0)

    def copy(k):
        return pltpu.make_async_copy(tok_ref.at[:, slab(idx_ref, k)], buf.at[k], sem.at[k])

    @pl.when(step == 0)
    def _():
        for k in range(n):
            copy(k).start()

    for k in range(n):

        @pl.when(step == k)
        def _(k=k):
            copy(k).wait()

    return buf[step]


def slab_scratch(n):
    return [pltpu.VMEM((n, ROWS, ROWS), BF16), pltpu.SemaphoreType.DMA((n,))]


def through(in_copies, out_copies):
    for copy in in_copies:
        copy.start()
    for copy, out in zip(in_copies, out_copies):
        copy.wait()
        out.start()
    for out in out_copies:
        out.wait()


def pack_first(tokens, cot, idx, after):
    def kernel(idx_ref, tok_ref, cot_ref, after_ref, out_ref, buf, sem, out_sem):
        del after_ref
        n, rows = 4, ROWS // 4
        ins, outs = [], []
        for i in range(n):
            part = pl.ds(i * rows, rows)
            tok_part, tok_buf = tok_ref.at[part, slab(idx_ref, 0)], buf.at[part, pl.ds(KV, ROWS)]
            ins.append(pltpu.make_async_copy(cot_ref.at[part], buf.at[part, pl.ds(0, KV)], sem.at[i]))
            ins.append(pltpu.make_async_copy(tok_part, tok_buf, sem.at[n + i]))
            outs.append(pltpu.make_async_copy(buf.at[part], out_ref.at[part], out_sem.at[i]))
        for copy in ins:
            copy.start()
        for i in range(n):
            ins[2 * i].wait()
            ins[2 * i + 1].wait()
            outs[i].start()
        for copy in outs:
            copy.wait()

    shape = (ROWS, KV + ROWS)
    return pl.pallas_call(
        kernel,
        grid_spec=pltpu.PrefetchScalarGridSpec(
            num_scalar_prefetch=1,
            grid=(1,),
            in_specs=[IN_HBM, ANYWHERE, ANYWHERE],
            out_specs=ANYWHERE,
            scratch_shapes=[
                pltpu.VMEM(shape, BF16),
                pltpu.SemaphoreType.DMA((8,)),
                pltpu.SemaphoreType.DMA((4,)),
            ],
        ),
        out_shape=jax.ShapeDtypeStruct(shape, BF16),
        name="pack_first",
        **params_of(0, 3 * 2**20, 58),
    )(idx, tokens, cot, after)


def unpack(target, pieces, idx):
    n = idx.shape[0]

    def kernel(idx_ref, old_ref, piece_ref, out_ref, buf, sem, out_sem):
        del old_ref
        through(
            [pltpu.make_async_copy(piece_ref.at[k], buf.at[k], sem.at[k]) for k in range(n)],
            [
                pltpu.make_async_copy(buf.at[k], out_ref.at[:, slab(idx_ref, k)], out_sem.at[k])
                for k in range(n)
            ],
        )

    return pl.pallas_call(
        kernel,
        grid_spec=pltpu.PrefetchScalarGridSpec(
            num_scalar_prefetch=1,
            grid=(1,),
            in_specs=[ANYWHERE] * 2,
            out_specs=ANYWHERE,
            scratch_shapes=[
                pltpu.VMEM((n, ROWS, ROWS), BF16),
                pltpu.SemaphoreType.DMA((n,)),
                pltpu.SemaphoreType.DMA((n,)),
            ],
        ),
        out_shape=jax.ShapeDtypeStruct(target.shape, BF16),
        input_output_aliases={1: 0},
        name="unpack",
        **params_of(0, n * 2**20, 58),
    )(idx, target, pieces)


def held_until(values, after):
    n, m = len(values), len(after)

    def kernel(*refs):
        del refs

    return pl.pallas_call(
        kernel,
        in_specs=[ANYWHERE] * (n + m),
        out_specs=[ANYWHERE] * n,
        out_shape=[jax.ShapeDtypeStruct(v.shape, v.dtype) for v in values],
        input_output_aliases={i: i for i in range(n)},
        name="held_until",
        **params_of(0, 0),
    )(*values, *after)


def gradients(tokens, other_tokens, cot, first, idx, cuts=None, after=()):
    n = idx.shape[0]
    if cuts is None:
        shapes = [(ROWS, KV)] * n
    else:
        shapes = [(hi - lo, KV) for lo, hi in cuts]

    def kernel(idx_ref, tok_ref, oth_ref, cot_ref, cot_oth_ref, *outs):
        outs = outs[len(after) :]
        outs, scratch = outs[: len(shapes)], outs[len(shapes) :]
        tok = token_slabs(idx_ref, tok_ref, *scratch[:2], n)
        step = pl.program_id(0)
        oth = oth_ref[...] if cuts is not None else token_slabs(idx_ref, oth_ref, *scratch[2:], n)
        total = dot(tok, cot_ref[...], TN) + dot(oth, cot_oth_ref[...], TN)
        total = (total * SCALE).astype(BF16)
        if cuts is not None:
            for (lo, hi), out in zip(cuts, outs):
                out[...] = total[lo:hi]
        else:
            for i, out in enumerate(outs):

                @pl.when(step == i)
                def _(out=out):
                    out[...] = total

    if cuts is not None:
        oth_spec = pl.BlockSpec((ROWS, ROWS), lambda k, idx: (0, KV // ROWS))
    else:
        oth_spec = IN_HBM
    return pl.pallas_call(
        kernel,
        grid_spec=pltpu.PrefetchScalarGridSpec(
            num_scalar_prefetch=1,
            grid=(n,),
            in_specs=[IN_HBM, oth_spec, whole((ROWS, KV)), whole((ROWS, KV))]
            + [ANYWHERE] * len(after),
            out_specs=[whole(s) for s in shapes],
            scratch_shapes=slab_scratch(n) * (1 if cuts is not None else 2),
        ),
        out_shape=[jax.ShapeDtypeStruct(s, BF16) for s in shapes],
        name="gradients",
        **params_of(n * 4 * ROWS * ROWS * KV, (2 * n + 2) * 2**20, 58),
    )(idx, tokens, other_tokens, cot, first, *after)


def forward(tokens, other_tokens, cot, first, weights, idx, after, keys=None, grad_in=None):
    n, m = idx.shape[0], len(after)
    last = keys is not None

    def kernel(idx_ref, tok_ref, oth_ref, cot_ref, cot_oth_ref, *refs):
        w_refs, rest = refs[:n], refs[n + m :]
        if last:
            own_in, oth_in, _, own_out, oth_out, gi_ref, back_ref, *rest, acc = rest
        else:
            own_out, oth_out, gi_ref, back_ref, *rest = rest
            acc = oth_out
        w_buf, sem, *slabs = rest
        step = pl.program_id(0)

        @pl.when(step == 0)
        def _():
            for i, w_ref in enumerate(w_refs):
                pltpu.make_async_copy(w_ref, w_buf.at[i], sem.at[i]).start()
            if last:
                own_out[...] = own_in[...]
                acc[...] = oth_in[...]
            else:
                own_out[...] = jnp.zeros_like(own_out)
                acc[...] = jnp.zeros_like(acc)

        for i, w_ref in enumerate(w_refs):

            @pl.when(step == i)
            def _(i=i, w_ref=w_ref):
                pltpu.make_async_copy(w_ref, w_buf.at[i], sem.at[i]).wait()

        w = w_buf[step]
        tok = token_slabs(idx_ref, tok_ref, *slabs[:2], n)
        oth = token_slabs(idx_ref, oth_ref, *slabs[2:], n)
        own_out[...] += dot(tok, w, NN)
        acc[...] += dot(oth, w, NN)
        gi_ref[...] = (dot(cot_ref[...], w, NT) * SCALE).astype(BF16)
        back_ref[0] = (dot(cot_oth_ref[...], w, NT) * SCALE).astype(BF16)

        if last:

            @pl.when(step == n - 1)
            def _():
                oth_out[...] = (acc[...] * SCALE).astype(BF16)

    in_specs = [IN_HBM, IN_HBM, whole((ROWS, KV)), whole((ROWS, KV))]
    in_specs += [ANYWHERE] * (n + m)
    operands = [tokens, other_tokens, cot, first, *weights, *after]
    aliases = {}
    scratch = [pltpu.VMEM((n, ROWS, KV), BF16), pltpu.SemaphoreType.DMA((n,)), *slab_scratch(n) * 2]
    if last:
        in_specs += [whole((ROWS, KV))] * 2 + [ANYWHERE]
        operands += [*keys, grad_in]
        aliases = {len(operands): 2}
        scratch += [pltpu.VMEM((ROWS, KV), F32)]
    return pl.pallas_call(
        kernel,
        grid_spec=pltpu.PrefetchScalarGridSpec(
            num_scalar_prefetch=1,
            grid=(n,),
            in_specs=in_specs,
            out_specs=[whole((ROWS, KV)), whole((ROWS, KV)), by_column(), by_step()],
            scratch_shapes=scratch,
        ),
        out_shape=[
            jax.ShapeDtypeStruct((ROWS, KV), F32),
            jax.ShapeDtypeStruct((ROWS, KV), BF16 if last else F32),
            jax.ShapeDtypeStruct((ROWS, D), BF16),
            jax.ShapeDtypeStruct((n, ROWS, ROWS), BF16),
        ],
        input_output_aliases=aliases,
        name="forward",
        **params_of(n * 8 * ROWS * ROWS * KV, (3 * n + 8) * 2**20, 36 if last else 58),
    )(idx, *operands)


def one_shard(tokens, cot, weights, keys, grad_in, idx, received=None):
    final = received is not None
    tile = ROWS // 2

    def kernel(idx_ref, tok_ref, cot_ref, w_ref, key_ref, *rest):
        *rest, tok_buf, sem = rest
        step, n = pl.program_id(0), ROWS // tile
        part = [pl.ds(i * tile, tile) for i in range(n)]
        copies = [
            pltpu.make_async_copy(tok_ref.at[p, slab(idx_ref, 0)], tok_buf.at[p], sem.at[i])
            for i, p in enumerate(part)
        ]

        @pl.when(step == 0)
        def _():
            for copy in copies:
                copy.start()

        for i, copy in enumerate(copies):

            @pl.when(step == i)
            def _(copy=copy):
                copy.wait()

        tok = tok_buf[pl.ds(pl.multiple_of(step * tile, tile), tile)]
        total = key_ref[...] + dot(tok, w_ref[...], NN)
        if final:
            rec_ref, _, key_out, gi_ref = rest
            key_out[...] = (total * SCALE + rec_ref[...].astype(F32)).astype(BF16)
        else:
            _, key_out, gi_ref = rest
            key_out[...] = total
        gi_ref[...] = (dot(cot_ref[...], w_ref[...], NT) * SCALE).astype(BF16)

    def wide():
        return pl.BlockSpec((tile, KV), lambda k, idx: (k, 0))

    def narrow():
        return pl.BlockSpec((tile, ROWS), lambda k, idx: (k, idx[0]))

    operands = [tokens, cot, weights, keys] + ([received] if final else []) + [grad_in]
    return pl.pallas_call(
        kernel,
        grid_spec=pltpu.PrefetchScalarGridSpec(
            num_scalar_prefetch=1,
            grid=(ROWS // tile,),
            in_specs=[IN_HBM, wide(), whole((ROWS, KV)), wide()]
            + ([wide()] if final else [])
            + [ANYWHERE],
            out_specs=[wide(), narrow()],
            scratch_shapes=[
                pltpu.VMEM((ROWS, ROWS), BF16),
                pltpu.SemaphoreType.DMA((ROWS // tile,)),
            ],
        ),
        out_shape=[
            jax.ShapeDtypeStruct((ROWS, KV), BF16 if final else F32),
            jax.ShapeDtypeStruct((ROWS, D), BF16),
        ],
        input_output_aliases={len(operands): 1},
        name="one_shard",
        **params_of(4 * ROWS * ROWS * KV, 8 * 2**20),
    )(idx, *operands)


def body(round_index, tokens, cotangent, params, momentum):
    tokens, cot, params, momentum = tokens[0], cotangent[0], params[0], momentum[0]
    bit = jnp.mod(round_index, LEVELS)
    half = ROWS // 2
    core = lax.axis_index("fsdp").astype(jnp.int32) % NC
    far, far_oth = columns(FAR, core), columns(FAR, 1 - core)
    mid, mid_oth = columns(MIDDLE, core), columns(MIDDLE, 1 - core)
    near, near_oth = columns(NEAR, core), columns(NEAR, 1 - core)
    rest = columns(MIDDLE + NEAR, core)

    own = params.astype(BF16)
    w_0m, w_01, w_10 = y_up(own), y_down(own), z_across(own)

    packed = pack_first(tokens, cot, far_oth, own)
    first = core_swap(packed)
    others = core_swap(tokens)

    t0, t1 = gradients(tokens, first, cot, first, far, cuts=((0, half), (half, ROWS)))
    (t1,) = held_until((t1,), (others,))
    t0, t1 = y_up(t0), y_down(t1)
    p_11, p_1m, p_02, p_0m, p_01, p_10, p_00 = gradients(
        tokens, others, cot, first, rest
    )
    p_11 = p_11.at[:half].add(t0)
    p_1m = p_1m.at[half:].add(t1)
    p_11, p_1m, p_02 = held_until((p_11, p_1m, p_02), (w_0m, w_01, w_10))
    key_own, key_oth, grad_in, back = forward(
        tokens, others, cot, first, (w_0m, w_01, w_10, own), near, (p_11, p_1m, p_02)
    )
    p_11, p_1m, p_02 = y_up(p_11), z_across(p_1m), y_down(p_02)
    p_0m = (p_0m.astype(F32) + p_1m.astype(F32) + p_02.astype(F32)).astype(BF16)
    p_10 = (p_10.astype(F32) + p_11.astype(F32)).astype(BF16)
    grad_in = unpack(grad_in, core_swap(back), near_oth)
    (p_01,) = held_until((p_01,), (key_own,))
    (own,) = held_until((own,), (p_0m, p_10, grad_in))
    p_0m, p_01, p_10 = y_down(p_0m), y_up(p_01), z_across(p_10)
    partner_params = partner_swap(own, bit)
    gradient = (p_00.astype(F32) + p_01.astype(F32)) + (p_0m.astype(F32) + p_10.astype(F32))
    moved = 0.9 * momentum + gradient

    w_0m, w_10 = held_until((w_0m, w_10), (p_0m, p_01, p_10, partner_params))
    w_02, w_11, w_1m = y_up(w_0m), y_down(w_10), z_across(w_0m)
    partner_moved = partner_swap(moved.astype(BF16), bit)
    pieces = w_1m[:half], w_11[half:]
    halves = y_up(pieces[0]), y_down(pieces[1])
    theirs = partner_moved.astype(F32)
    new_momentum = 0.5 * (moved + theirs)
    partner_stepped = partner_params.astype(F32) - 0.1 * theirs
    new_params = 0.5 * ((params - 0.1 * moved) + partner_stepped)
    key_own, key_oth, grad_in, back = forward(
        tokens,
        others,
        cot,
        first,
        (w_11, w_1m, w_02),
        mid,
        (partner_moved, *pieces),
        (key_own, key_oth),
        grad_in,
    )
    key_oth = core_swap(key_oth)
    (w_12,) = held_until((jnp.concatenate(halves, axis=0),), (new_params, new_momentum))
    w_12_oth = core_swap(w_12)
    grad_in = unpack(grad_in, core_swap(back), mid_oth)
    key_own, grad_in = one_shard(tokens, cot, w_12, key_own, grad_in, far)
    key_out, grad_in = one_shard(tokens, cot, w_12_oth, key_own, grad_in, far_oth, key_oth)
    return key_out[None], grad_in[None], new_params[None], new_momentum[None]


def solution(mesh):
    rows = P("rep", "fsdp", None)
    return jax.shard_map(
        body,
        mesh=mesh,
        in_specs=(P(), rows, rows, rows, rows),
        out_specs=(rows, rows, rows, rows),
        check_vma=False,
    )
```

```python
import jax
import jax.numpy as jnp
from jax import lax
from jax.experimental import pallas as pl
from jax.experimental.pallas import tpu as pltpu
from jax.sharding import PartitionSpec as P

D = 8192
KV = 1024
ROWS = 512
NZ, NY, NC = 2, 4, 2
SCALE = D ** (-0.5)
LEVELS = 3
TN = (((0,), (0,)), ((), ()))
NT = (((1,), (1,)), ((), ()))
NN = (((1,), (0,)), ((), ()))
F32, BF16 = jnp.float32, jnp.bfloat16

FAR = ((1, 2),)
MIDDLE = ((1, 1), (1, -1), (0, 2))
NEAR = ((0, -1), (0, 1), (1, 0), (0, 0))


def place(z, y, c):
    return (z % NZ) * NY * NC + (y % NY) * NC + c % NC


def shift(dz=0, dy=0, dc=0):
    return [
        (place(z, y, c), place(z + dz, y + dy, c + dc))
        for z in range(NZ)
        for y in range(NY)
        for c in range(NC)
    ]


def y_up(value):
    return lax.ppermute(value, "fsdp", shift(dy=1))


def y_down(value):
    return lax.ppermute(value, "fsdp", shift(dy=-1))


def z_across(value):
    return lax.ppermute(value, "fsdp", shift(dz=1))


def core_swap(value):
    return lax.ppermute(value, "fsdp", shift(dc=1))


def partner_swap(value, bit):
    def swap(arr, level):
        return lax.ppermute(arr, "rep", [(r, r ^ (1 << level)) for r in range(1 << LEVELS)])

    return lax.switch(bit, [lambda arr, level=level: swap(arr, level) for level in range(LEVELS)], value)


def columns(offsets, core):
    f = lax.axis_index("fsdp").astype(jnp.int32)
    z, y = f // (NY * NC), (f // NC) % NY
    return jnp.stack([place(z + dz, y + dy, core).astype(jnp.int32) for dz, dy in offsets])


def dot(a, b, dims):
    return lax.dot_general(a, b, dims, preferred_element_type=F32)


def whole(shape):
    return pl.BlockSpec(shape, lambda k, idx: (0,) * len(shape))


def by_column():
    return pl.BlockSpec((ROWS, ROWS), lambda k, idx: (0, idx[k]))


def by_step():
    return pl.BlockSpec((1, ROWS, ROWS), lambda k, idx: (k, 0, 0))


def params_of(flops, nbytes, vmem=36):
    flops, nbytes = int(flops), int(nbytes)
    return dict(
        compiler_params=pltpu.CompilerParams(vmem_limit_bytes=vmem * 2**20),
        cost_estimate=pl.CostEstimate(flops=flops, bytes_accessed=nbytes, transcendentals=0),
    )


ANYWHERE = pl.BlockSpec(memory_space=pl.ANY)
IN_HBM = pl.BlockSpec(memory_space=pltpu.HBM)


def slab(idx_ref, k):
    return pl.ds(pl.multiple_of(idx_ref[k] * ROWS, ROWS), ROWS)


def token_slabs(idx_ref, tok_ref, buf, sem, n):
    step = pl.program_id(0)

    def copy(k):
        return pltpu.make_async_copy(tok_ref.at[:, slab(idx_ref, k)], buf.at[k], sem.at[k])

    @pl.when(step == 0)
    def _():
        for k in range(n):
            copy(k).start()

    for k in range(n):

        @pl.when(step == k)
        def _(k=k):
            copy(k).wait()

    return buf[step]


def slab_scratch(n):
    return [pltpu.VMEM((n, ROWS, ROWS), BF16), pltpu.SemaphoreType.DMA((n,))]


def through(in_copies, out_copies):
    for copy in in_copies:
        copy.start()
    for copy, out in zip(in_copies, out_copies):
        copy.wait()
        out.start()
    for out in out_copies:
        out.wait()


def pack_first(tokens, cot, idx, after):
    def kernel(idx_ref, tok_ref, cot_ref, after_ref, out_ref, buf, sem, out_sem):
        del after_ref
        n, rows = 4, ROWS // 4
        ins, outs = [], []
        for i in range(n):
            part = pl.ds(i * rows, rows)
            tok_part, tok_buf = tok_ref.at[part, slab(idx_ref, 0)], buf.at[part, pl.ds(KV, ROWS)]
            ins.append(pltpu.make_async_copy(cot_ref.at[part], buf.at[part, pl.ds(0, KV)], sem.at[i]))
            ins.append(pltpu.make_async_copy(tok_part, tok_buf, sem.at[n + i]))
            outs.append(pltpu.make_async_copy(buf.at[part], out_ref.at[part], out_sem.at[i]))
        for copy in ins:
            copy.start()
        for i in range(n):
            ins[2 * i].wait()
            ins[2 * i + 1].wait()
            outs[i].start()
        for copy in outs:
            copy.wait()

    shape = (ROWS, KV + ROWS)
    return pl.pallas_call(
        kernel,
        grid_spec=pltpu.PrefetchScalarGridSpec(
            num_scalar_prefetch=1,
            grid=(1,),
            in_specs=[IN_HBM, ANYWHERE, ANYWHERE],
            out_specs=ANYWHERE,
            scratch_shapes=[
                pltpu.VMEM(shape, BF16),
                pltpu.SemaphoreType.DMA((8,)),
                pltpu.SemaphoreType.DMA((4,)),
            ],
        ),
        out_shape=jax.ShapeDtypeStruct(shape, BF16),
        name="pack_first",
        **params_of(0, 3 * 2**20, 58),
    )(idx, tokens, cot, after)


def unpack(target, pieces, idx):
    n = idx.shape[0]

    def kernel(idx_ref, old_ref, piece_ref, out_ref, buf, sem, out_sem):
        del old_ref
        through(
            [pltpu.make_async_copy(piece_ref.at[k], buf.at[k], sem.at[k]) for k in range(n)],
            [
                pltpu.make_async_copy(buf.at[k], out_ref.at[:, slab(idx_ref, k)], out_sem.at[k])
                for k in range(n)
            ],
        )

    return pl.pallas_call(
        kernel,
        grid_spec=pltpu.PrefetchScalarGridSpec(
            num_scalar_prefetch=1,
            grid=(1,),
            in_specs=[ANYWHERE] * 2,
            out_specs=ANYWHERE,
            scratch_shapes=[
                pltpu.VMEM((n, ROWS, ROWS), BF16),
                pltpu.SemaphoreType.DMA((n,)),
                pltpu.SemaphoreType.DMA((n,)),
            ],
        ),
        out_shape=jax.ShapeDtypeStruct(target.shape, BF16),
        input_output_aliases={1: 0},
        name="unpack",
        **params_of(0, n * 2**20, 58),
    )(idx, target, pieces)


def held_until(values, after):
    after = [array[:16, :128] if array.size > ROWS * KV or array.dtype == F32 else array for array in after]
    n, m = len(values), len(after)

    def kernel(*refs):
        del refs

    return pl.pallas_call(
        kernel,
        in_specs=[ANYWHERE] * (n + m),
        out_specs=[ANYWHERE] * n,
        out_shape=[jax.ShapeDtypeStruct(v.shape, v.dtype) for v in values],
        input_output_aliases={i: i for i in range(n)},
        name="held_until",
        **params_of(0, 0),
    )(*values, *after)


def gradients(tokens, other_tokens, cot, first, idx, cuts=None, after=()):
    n = idx.shape[0]
    if cuts is None:
        shapes = [(ROWS, KV)] * n
    else:
        shapes = [(hi - lo, KV) for lo, hi in cuts]

    def kernel(idx_ref, tok_ref, oth_ref, cot_ref, cot_oth_ref, *outs):
        outs = outs[len(after) :]
        outs, scratch = outs[: len(shapes)], outs[len(shapes) :]
        tok = token_slabs(idx_ref, tok_ref, *scratch[:2], n)
        step = pl.program_id(0)
        oth = oth_ref[...] if cuts is not None else token_slabs(idx_ref, oth_ref, *scratch[2:], n)
        total = dot(tok, cot_ref[...], TN) + dot(oth, cot_oth_ref[...], TN)
        total = (total * SCALE).astype(BF16)
        if cuts is not None:
            for (lo, hi), out in zip(cuts, outs):
                out[...] = total[lo:hi]
        else:
            for i, out in enumerate(outs):

                @pl.when(step == i)
                def _(out=out):
                    out[...] = total

    if cuts is not None:
        oth_spec = pl.BlockSpec((ROWS, ROWS), lambda k, idx: (0, KV // ROWS))
    else:
        oth_spec = IN_HBM
    return pl.pallas_call(
        kernel,
        grid_spec=pltpu.PrefetchScalarGridSpec(
            num_scalar_prefetch=1,
            grid=(n,),
            in_specs=[IN_HBM, oth_spec, whole((ROWS, KV)), whole((ROWS, KV))]
            + [ANYWHERE] * len(after),
            out_specs=[whole(s) for s in shapes],
            scratch_shapes=slab_scratch(n) * (1 if cuts is not None else 2),
        ),
        out_shape=[jax.ShapeDtypeStruct(s, BF16) for s in shapes],
        name="gradients",
        **params_of(n * 4 * ROWS * ROWS * KV, (2 * n + 2) * 2**20, 58 if n == 1 else 36),
    )(idx, tokens, other_tokens, cot, first, *after)


def forward(tokens, other_tokens, cot, first, weights, idx, after, keys=None, grad_in=None):
    n, m = idx.shape[0], len(after)
    last = keys is not None

    def kernel(idx_ref, tok_ref, oth_ref, cot_ref, cot_oth_ref, *refs):
        w_refs, rest = refs[:n], refs[n + m :]
        if last:
            own_in, oth_in, _, own_out, oth_out, gi_ref, back_ref, *rest, acc = rest
        else:
            own_out, oth_out, gi_ref, back_ref, *rest = rest
            acc = oth_out
        w_buf, sem, *slabs = rest
        step = pl.program_id(0)

        @pl.when(step == 0)
        def _():
            for i, w_ref in enumerate(w_refs):
                pltpu.make_async_copy(w_ref, w_buf.at[i], sem.at[i]).start()
            if last:
                own_out[...] = own_in[...]
                acc[...] = oth_in[...]
            else:
                own_out[...] = jnp.zeros_like(own_out)
                acc[...] = jnp.zeros_like(acc)

        for i, w_ref in enumerate(w_refs):

            @pl.when(step == i)
            def _(i=i, w_ref=w_ref):
                pltpu.make_async_copy(w_ref, w_buf.at[i], sem.at[i]).wait()

        w = w_buf[step]
        tok = token_slabs(idx_ref, tok_ref, *slabs[:2], n)
        oth = token_slabs(idx_ref, oth_ref, *slabs[2:], n)
        own_out[...] += dot(tok, w, NN)
        acc[...] += dot(oth, w, NN)
        gi_ref[...] = (dot(cot_ref[...], w, NT) * SCALE).astype(BF16)
        back_ref[0] = (dot(cot_oth_ref[...], w, NT) * SCALE).astype(BF16)

        if last:

            @pl.when(step == n - 1)
            def _():
                oth_out[...] = (acc[...] * SCALE).astype(BF16)

    in_specs = [IN_HBM, IN_HBM, whole((ROWS, KV)), whole((ROWS, KV))]
    in_specs += [ANYWHERE] * (n + m)
    operands = [tokens, other_tokens, cot, first, *weights, *after]
    aliases = {}
    scratch = [pltpu.VMEM((n, ROWS, KV), BF16), pltpu.SemaphoreType.DMA((n,)), *slab_scratch(n) * 2]
    if last:
        in_specs += [whole((ROWS, KV))] * 2 + [ANYWHERE]
        operands += [*keys, grad_in]
        aliases = {len(operands): 2}
        scratch += [pltpu.VMEM((ROWS, KV), F32)]
    return pl.pallas_call(
        kernel,
        grid_spec=pltpu.PrefetchScalarGridSpec(
            num_scalar_prefetch=1,
            grid=(n,),
            in_specs=in_specs,
            out_specs=[whole((ROWS, KV)), whole((ROWS, KV)), by_column(), by_step()],
            scratch_shapes=scratch,
        ),
        out_shape=[
            jax.ShapeDtypeStruct((ROWS, KV), F32),
            jax.ShapeDtypeStruct((ROWS, KV), BF16 if last else F32),
            jax.ShapeDtypeStruct((ROWS, D), BF16),
            jax.ShapeDtypeStruct((n, ROWS, ROWS), BF16),
        ],
        input_output_aliases=aliases,
        name="forward",
        **params_of(n * 8 * ROWS * ROWS * KV, (3 * n + 8) * 2**20),
    )(idx, *operands)


def one_shard(tokens, cot, weights, keys, grad_in, idx, received=None):
    final = received is not None
    tile = ROWS // 2

    def kernel(idx_ref, tok_ref, cot_ref, w_ref, key_ref, *rest):
        *rest, tok_buf, sem = rest
        step, n = pl.program_id(0), ROWS // tile
        part = [pl.ds(i * tile, tile) for i in range(n)]
        copies = [
            pltpu.make_async_copy(tok_ref.at[p, slab(idx_ref, 0)], tok_buf.at[p], sem.at[i])
            for i, p in enumerate(part)
        ]

        @pl.when(step == 0)
        def _():
            for copy in copies:
                copy.start()

        for i, copy in enumerate(copies):

            @pl.when(step == i)
            def _(copy=copy):
                copy.wait()

        tok = tok_buf[pl.ds(pl.multiple_of(step * tile, tile), tile)]
        total = key_ref[...] + dot(tok, w_ref[...], NN)
        if final:
            rec_ref, _, key_out, gi_ref = rest
            key_out[...] = (total * SCALE + rec_ref[...].astype(F32)).astype(BF16)
        else:
            _, key_out, gi_ref = rest
            key_out[...] = total
        gi_ref[...] = (dot(cot_ref[...], w_ref[...], NT) * SCALE).astype(BF16)

    def wide():
        return pl.BlockSpec((tile, KV), lambda k, idx: (k, 0))

    def narrow():
        return pl.BlockSpec((tile, ROWS), lambda k, idx: (k, idx[0]))

    operands = [tokens, cot, weights, keys] + ([received] if final else []) + [grad_in]
    return pl.pallas_call(
        kernel,
        grid_spec=pltpu.PrefetchScalarGridSpec(
            num_scalar_prefetch=1,
            grid=(ROWS // tile,),
            in_specs=[IN_HBM, wide(), whole((ROWS, KV)), wide()]
            + ([wide()] if final else [])
            + [ANYWHERE],
            out_specs=[wide(), narrow()],
            scratch_shapes=[
                pltpu.VMEM((ROWS, ROWS), BF16),
                pltpu.SemaphoreType.DMA((ROWS // tile,)),
            ],
        ),
        out_shape=[
            jax.ShapeDtypeStruct((ROWS, KV), BF16 if final else F32),
            jax.ShapeDtypeStruct((ROWS, D), BF16),
        ],
        input_output_aliases={len(operands): 1},
        name="one_shard",
        **params_of(4 * ROWS * ROWS * KV, 8 * 2**20),
    )(idx, *operands)


def body(round_index, tokens, cotangent, params, momentum):
    tokens, cot, params, momentum = tokens[0], cotangent[0], params[0], momentum[0]
    bit = jnp.mod(round_index, LEVELS)
    half = ROWS // 2
    core = lax.axis_index("fsdp").astype(jnp.int32) % NC
    far, far_oth = columns(FAR, core), columns(FAR, 1 - core)
    mid, mid_oth = columns(MIDDLE, core), columns(MIDDLE, 1 - core)
    near, near_oth = columns(NEAR, core), columns(NEAR, 1 - core)
    rest = columns(MIDDLE + NEAR, core)

    own = params.astype(BF16)
    w_0m, w_01, w_10 = y_up(own), y_down(own), z_across(own)

    packed = pack_first(tokens, cot, far_oth, own)
    first = core_swap(packed)
    others = core_swap(tokens)

    t0, t1 = gradients(tokens, first, cot, first, far, cuts=((0, half), (half, ROWS)))
    (t1,) = held_until((t1,), (others,))
    t0, t1 = y_up(t0), y_down(t1)
    p_11, p_1m, p_02, p_0m, p_01, p_10, p_00 = gradients(
        tokens, others, cot, first, rest
    )
    p_11 = p_11.at[:half].add(t0)
    p_1m = p_1m.at[half:].add(t1)
    p_11, p_1m, p_02 = held_until((p_11, p_1m, p_02), (w_0m, w_01, w_10))
    key_own, key_oth, grad_in, back = forward(
        tokens, others, cot, first, (w_0m, w_01, w_10, own), near, (p_11, p_1m, p_02)
    )
    p_11, p_1m, p_02 = y_up(p_11), z_across(p_1m), y_down(p_02)
    p_0m = (p_0m.astype(F32) + p_1m.astype(F32) + p_02.astype(F32)).astype(BF16)
    p_10 = (p_10.astype(F32) + p_11.astype(F32)).astype(BF16)
    grad_in = unpack(grad_in, core_swap(back), near_oth)
    (p_01,) = held_until((p_01,), (key_own,))
    (own,) = held_until((own,), (p_0m, p_10, grad_in))
    p_0m, p_01, p_10 = y_down(p_0m), y_up(p_01), z_across(p_10)
    partner_params = partner_swap(own, bit)
    gradient = (p_00.astype(F32) + p_01.astype(F32)) + (p_0m.astype(F32) + p_10.astype(F32))
    moved = 0.9 * momentum + gradient

    w_0m, w_10 = held_until((w_0m, w_10), (p_0m, p_01, p_10, partner_params))
    w_02, w_11, w_1m = y_up(w_0m), y_down(w_10), z_across(w_0m)
    partner_moved = partner_swap(moved.astype(BF16), bit)
    pieces = w_1m[:half], w_11[half:]
    halves = y_up(pieces[0]), y_down(pieces[1])
    theirs = partner_moved.astype(F32)
    new_momentum = 0.5 * (moved + theirs)
    partner_stepped = partner_params.astype(F32) - 0.1 * theirs
    new_params = 0.5 * ((params - 0.1 * moved) + partner_stepped)
    key_own, key_oth, grad_in, back = forward(
        tokens,
        others,
        cot,
        first,
        (w_11, w_1m, w_02),
        mid,
        (partner_moved, *pieces),
        (key_own, key_oth),
        grad_in,
    )
    key_oth = core_swap(key_oth)
    (w_12,) = held_until((jnp.concatenate(halves, axis=0),), (new_params, new_momentum))
    w_12_oth = core_swap(w_12)
    grad_in = unpack(grad_in, core_swap(back), mid_oth)
    key_own, grad_in = one_shard(tokens, cot, w_12, key_own, grad_in, far)
    key_out, grad_in = one_shard(tokens, cot, w_12_oth, key_own, grad_in, far_oth, key_oth)
    return key_out[None], grad_in[None], new_params[None], new_momentum[None]


def solution(mesh):
    rows = P("rep", "fsdp", None)
    return jax.shard_map(
        body,
        mesh=mesh,
        in_specs=(P(), rows, rows, rows, rows),
        out_specs=(rows, rows, rows, rows),
        check_vma=False,
    )
```

```python
import jax
import jax.numpy as jnp
from jax import lax
from jax.experimental import pallas as pl
from jax.experimental.pallas import tpu as pltpu
from jax.sharding import PartitionSpec as P

D = 8192
KV = 1024
ROWS = 512
NZ, NY, NC = 2, 4, 2
SCALE = D ** (-0.5)
LEVELS = 3
TN = (((0,), (0,)), ((), ()))
NT = (((1,), (1,)), ((), ()))
NN = (((1,), (0,)), ((), ()))
F32, BF16 = jnp.float32, jnp.bfloat16

FAR = ((1, 2),)
MIDDLE = ((1, 1), (1, -1), (0, 2))
NEAR = ((0, -1), (0, 1), (1, 0), (0, 0))


def place(z, y, c):
    return (z % NZ) * NY * NC + (y % NY) * NC + c % NC


def shift(dz=0, dy=0, dc=0):
    return [
        (place(z, y, c), place(z + dz, y + dy, c + dc))
        for z in range(NZ)
        for y in range(NY)
        for c in range(NC)
    ]


def y_up(value):
    return lax.ppermute(value, "fsdp", shift(dy=1))


def y_down(value):
    return lax.ppermute(value, "fsdp", shift(dy=-1))


def z_across(value):
    return lax.ppermute(value, "fsdp", shift(dz=1))


def core_swap(value):
    return lax.ppermute(value, "fsdp", shift(dc=1))


def partner_swap(value, bit):
    def swap(arr, level):
        return lax.ppermute(arr, "rep", [(r, r ^ (1 << level)) for r in range(1 << LEVELS)])

    return lax.switch(bit, [lambda arr, level=level: swap(arr, level) for level in range(LEVELS)], value)


def columns(offsets, core):
    f = lax.axis_index("fsdp").astype(jnp.int32)
    z, y = f // (NY * NC), (f // NC) % NY
    return jnp.stack([place(z + dz, y + dy, core).astype(jnp.int32) for dz, dy in offsets])


def dot(a, b, dims):
    return lax.dot_general(a, b, dims, preferred_element_type=F32)


def whole(shape):
    return pl.BlockSpec(shape, lambda k, idx: (0,) * len(shape))


def by_column():
    return pl.BlockSpec((ROWS, ROWS), lambda k, idx: (0, idx[k]))


def by_step():
    return pl.BlockSpec((1, ROWS, ROWS), lambda k, idx: (k, 0, 0))


def params_of(flops, nbytes, vmem=36):
    flops, nbytes = int(flops), int(nbytes)
    return dict(
        compiler_params=pltpu.CompilerParams(vmem_limit_bytes=vmem * 2**20),
        cost_estimate=pl.CostEstimate(flops=flops, bytes_accessed=nbytes, transcendentals=0),
    )


ANYWHERE = pl.BlockSpec(memory_space=pl.ANY)
IN_HBM = pl.BlockSpec(memory_space=pltpu.HBM)


def slab(idx_ref, k):
    return pl.ds(pl.multiple_of(idx_ref[k] * ROWS, ROWS), ROWS)


def token_slabs(idx_ref, tok_ref, buf, sem, n):
    step = pl.program_id(0)

    def copy(k):
        return pltpu.make_async_copy(tok_ref.at[:, slab(idx_ref, k)], buf.at[k], sem.at[k])

    @pl.when(step == 0)
    def _():
        for k in range(n):
            copy(k).start()

    for k in range(n):

        @pl.when(step == k)
        def _(k=k):
            copy(k).wait()

    return buf[step]


def slab_scratch(n):
    return [pltpu.VMEM((n, ROWS, ROWS), BF16), pltpu.SemaphoreType.DMA((n,))]


def through(in_copies, out_copies):
    for copy in in_copies:
        copy.start()
    for copy, out in zip(in_copies, out_copies):
        copy.wait()
        out.start()
    for out in out_copies:
        out.wait()


def pack_first(tokens, cot, idx, after):
    def kernel(idx_ref, tok_ref, cot_ref, after_ref, out_ref, buf, sem, out_sem):
        del after_ref
        n, rows = 4, ROWS // 4
        ins, outs = [], []
        for i in range(n):
            part = pl.ds(i * rows, rows)
            tok_part, tok_buf = tok_ref.at[part, slab(idx_ref, 0)], buf.at[part, pl.ds(KV, ROWS)]
            ins.append(pltpu.make_async_copy(cot_ref.at[part], buf.at[part, pl.ds(0, KV)], sem.at[i]))
            ins.append(pltpu.make_async_copy(tok_part, tok_buf, sem.at[n + i]))
            outs.append(pltpu.make_async_copy(buf.at[part], out_ref.at[part], out_sem.at[i]))
        for copy in ins:
            copy.start()
        for i in range(n):
            ins[2 * i].wait()
            ins[2 * i + 1].wait()
            outs[i].start()
        for copy in outs:
            copy.wait()

    shape = (ROWS, KV + ROWS)
    return pl.pallas_call(
        kernel,
        grid_spec=pltpu.PrefetchScalarGridSpec(
            num_scalar_prefetch=1,
            grid=(1,),
            in_specs=[IN_HBM, ANYWHERE, ANYWHERE],
            out_specs=ANYWHERE,
            scratch_shapes=[
                pltpu.VMEM(shape, BF16),
                pltpu.SemaphoreType.DMA((8,)),
                pltpu.SemaphoreType.DMA((4,)),
            ],
        ),
        out_shape=jax.ShapeDtypeStruct(shape, BF16),
        name="pack_first",
        **params_of(0, 3 * 2**20, 58),
    )(idx, tokens, cot, after)


def unpack(target, pieces, idx):
    n = idx.shape[0]

    def kernel(idx_ref, old_ref, piece_ref, out_ref, buf, sem, out_sem):
        del old_ref
        through(
            [pltpu.make_async_copy(piece_ref.at[k], buf.at[k], sem.at[k]) for k in range(n)],
            [
                pltpu.make_async_copy(buf.at[k], out_ref.at[:, slab(idx_ref, k)], out_sem.at[k])
                for k in range(n)
            ],
        )

    return pl.pallas_call(
        kernel,
        grid_spec=pltpu.PrefetchScalarGridSpec(
            num_scalar_prefetch=1,
            grid=(1,),
            in_specs=[ANYWHERE] * 2,
            out_specs=ANYWHERE,
            scratch_shapes=[
                pltpu.VMEM((n, ROWS, ROWS), BF16),
                pltpu.SemaphoreType.DMA((n,)),
                pltpu.SemaphoreType.DMA((n,)),
            ],
        ),
        out_shape=jax.ShapeDtypeStruct(target.shape, BF16),
        input_output_aliases={1: 0},
        name="unpack",
        **params_of(0, n * 2**20),
    )(idx, target, pieces)


def held_until(values, after):
    after = [array[:16, :128] if array.size > ROWS * KV or array.dtype == F32 else array for array in after]
    n, m = len(values), len(after)

    def kernel(*refs):
        del refs

    return pl.pallas_call(
        kernel,
        in_specs=[ANYWHERE] * (n + m),
        out_specs=[ANYWHERE] * n,
        out_shape=[jax.ShapeDtypeStruct(v.shape, v.dtype) for v in values],
        input_output_aliases={i: i for i in range(n)},
        name="held_until",
        **params_of(0, 0),
    )(*values, *after)


def gradients(tokens, other_tokens, cot, first, idx, cuts=None, after=()):
    n = idx.shape[0]
    if cuts is None:
        shapes = [(ROWS, KV)] * n
    else:
        shapes = [(hi - lo, KV) for lo, hi in cuts]

    def kernel(idx_ref, tok_ref, oth_ref, cot_ref, cot_oth_ref, *outs):
        outs = outs[len(after) :]
        outs, scratch = outs[: len(shapes)], outs[len(shapes) :]
        tok = token_slabs(idx_ref, tok_ref, *scratch[:2], n)
        step = pl.program_id(0)
        oth = oth_ref[...] if cuts is not None else token_slabs(idx_ref, oth_ref, *scratch[2:], n)
        total = dot(tok, cot_ref[...], TN) + dot(oth, cot_oth_ref[...], TN)
        total = (total * SCALE).astype(BF16)
        if cuts is not None:
            for (lo, hi), out in zip(cuts, outs):
                out[...] = total[lo:hi]
        else:
            for i, out in enumerate(outs):

                @pl.when(step == i)
                def _(out=out):
                    out[...] = total

    if cuts is not None:
        oth_spec = pl.BlockSpec((ROWS, ROWS), lambda k, idx: (0, KV // ROWS))
    else:
        oth_spec = IN_HBM
    return pl.pallas_call(
        kernel,
        grid_spec=pltpu.PrefetchScalarGridSpec(
            num_scalar_prefetch=1,
            grid=(n,),
            in_specs=[IN_HBM, oth_spec, whole((ROWS, KV)), whole((ROWS, KV))]
            + [ANYWHERE] * len(after),
            out_specs=[whole(s) for s in shapes],
            scratch_shapes=slab_scratch(n) * (1 if cuts is not None else 2),
        ),
        out_shape=[jax.ShapeDtypeStruct(s, BF16) for s in shapes],
        name="gradients",
        **params_of(n * 4 * ROWS * ROWS * KV, (2 * n + 2) * 2**20, 58 if n == 1 else 36),
    )(idx, tokens, other_tokens, cot, first, *after)


def forward(tokens, other_tokens, cot, first, weights, idx, after, keys=None, grad_in=None):
    n, m = idx.shape[0], len(after)
    last = keys is not None

    def kernel(idx_ref, tok_ref, oth_ref, cot_ref, cot_oth_ref, *refs):
        w_refs, rest = refs[:n], refs[n + m :]
        if last:
            own_in, oth_in, _, own_out, oth_out, gi_ref, back_ref, *rest, acc = rest
        else:
            own_out, oth_out, gi_ref, back_ref, *rest = rest
            acc = oth_out
        w_buf, sem, *slabs = rest
        step = pl.program_id(0)

        @pl.when(step == 0)
        def _():
            for i, w_ref in enumerate(w_refs):
                pltpu.make_async_copy(w_ref, w_buf.at[i], sem.at[i]).start()
            if last:
                own_out[...] = own_in[...]
                acc[...] = oth_in[...]
            else:
                own_out[...] = jnp.zeros_like(own_out)
                acc[...] = jnp.zeros_like(acc)

        for i, w_ref in enumerate(w_refs):

            @pl.when(step == i)
            def _(i=i, w_ref=w_ref):
                pltpu.make_async_copy(w_ref, w_buf.at[i], sem.at[i]).wait()

        w = w_buf[step]
        tok = token_slabs(idx_ref, tok_ref, *slabs[:2], n)
        oth = token_slabs(idx_ref, oth_ref, *slabs[2:], n)
        own_out[...] += dot(tok, w, NN)
        acc[...] += dot(oth, w, NN)
        gi_ref[...] = (dot(cot_ref[...], w, NT) * SCALE).astype(BF16)
        back_ref[0] = (dot(cot_oth_ref[...], w, NT) * SCALE).astype(BF16)

        if last:

            @pl.when(step == n - 1)
            def _():
                oth_out[...] = (acc[...] * SCALE).astype(BF16)

    in_specs = [IN_HBM, IN_HBM, whole((ROWS, KV)), whole((ROWS, KV))]
    in_specs += [ANYWHERE] * (n + m)
    operands = [tokens, other_tokens, cot, first, *weights, *after]
    aliases = {}
    scratch = [pltpu.VMEM((n, ROWS, KV), BF16), pltpu.SemaphoreType.DMA((n,)), *slab_scratch(n) * 2]
    if last:
        in_specs += [whole((ROWS, KV))] * 2 + [ANYWHERE]
        operands += [*keys, grad_in]
        aliases = {len(operands): 2}
        scratch += [pltpu.VMEM((ROWS, KV), F32)]
    return pl.pallas_call(
        kernel,
        grid_spec=pltpu.PrefetchScalarGridSpec(
            num_scalar_prefetch=1,
            grid=(n,),
            in_specs=in_specs,
            out_specs=[whole((ROWS, KV)), whole((ROWS, KV)), by_column(), by_step()],
            scratch_shapes=scratch,
        ),
        out_shape=[
            jax.ShapeDtypeStruct((ROWS, KV), F32),
            jax.ShapeDtypeStruct((ROWS, KV), BF16 if last else F32),
            jax.ShapeDtypeStruct((ROWS, D), BF16),
            jax.ShapeDtypeStruct((n, ROWS, ROWS), BF16),
        ],
        input_output_aliases=aliases,
        name="forward",
        **params_of(n * 8 * ROWS * ROWS * KV, (3 * n + 8) * 2**20),
    )(idx, *operands)


def one_shard(tokens, cot, weights, keys, grad_in, idx, received=None):
    final = received is not None
    tile = ROWS // 2

    def kernel(idx_ref, tok_ref, cot_ref, w_ref, key_ref, *rest):
        *rest, tok_buf, sem = rest
        step, n = pl.program_id(0), ROWS // tile
        part = [pl.ds(i * tile, tile) for i in range(n)]
        copies = [
            pltpu.make_async_copy(tok_ref.at[p, slab(idx_ref, 0)], tok_buf.at[p], sem.at[i])
            for i, p in enumerate(part)
        ]

        @pl.when(step == 0)
        def _():
            for copy in copies:
                copy.start()

        for i, copy in enumerate(copies):

            @pl.when(step == i)
            def _(copy=copy):
                copy.wait()

        tok = tok_buf[pl.ds(pl.multiple_of(step * tile, tile), tile)]
        total = key_ref[...] + dot(tok, w_ref[...], NN)
        if final:
            rec_ref, _, key_out, gi_ref = rest
            key_out[...] = (total * SCALE + rec_ref[...].astype(F32)).astype(BF16)
        else:
            _, key_out, gi_ref = rest
            key_out[...] = total
        gi_ref[...] = (dot(cot_ref[...], w_ref[...], NT) * SCALE).astype(BF16)

    def wide():
        return pl.BlockSpec((tile, KV), lambda k, idx: (k, 0))

    def narrow():
        return pl.BlockSpec((tile, ROWS), lambda k, idx: (k, idx[0]))

    operands = [tokens, cot, weights, keys] + ([received] if final else []) + [grad_in]
    return pl.pallas_call(
        kernel,
        grid_spec=pltpu.PrefetchScalarGridSpec(
            num_scalar_prefetch=1,
            grid=(ROWS // tile,),
            in_specs=[IN_HBM, wide(), whole((ROWS, KV)), wide()]
            + ([wide()] if final else [])
            + [ANYWHERE],
            out_specs=[wide(), narrow()],
            scratch_shapes=[
                pltpu.VMEM((ROWS, ROWS), BF16),
                pltpu.SemaphoreType.DMA((ROWS // tile,)),
            ],
        ),
        out_shape=[
            jax.ShapeDtypeStruct((ROWS, KV), BF16 if final else F32),
            jax.ShapeDtypeStruct((ROWS, D), BF16),
        ],
        input_output_aliases={len(operands): 1},
        name="one_shard",
        **params_of(4 * ROWS * ROWS * KV, 8 * 2**20, 57),
    )(idx, *operands)


def body(round_index, tokens, cotangent, params, momentum):
    tokens, cot, params, momentum = tokens[0], cotangent[0], params[0], momentum[0]
    bit = jnp.mod(round_index, LEVELS)
    half = ROWS // 2
    core = lax.axis_index("fsdp").astype(jnp.int32) % NC
    far, far_oth = columns(FAR, core), columns(FAR, 1 - core)
    mid, mid_oth = columns(MIDDLE, core), columns(MIDDLE, 1 - core)
    near, near_oth = columns(NEAR, core), columns(NEAR, 1 - core)
    rest = columns(MIDDLE + NEAR, core)

    own = params.astype(BF16)
    w_0m, w_01, w_10 = y_up(own), y_down(own), z_across(own)

    packed = pack_first(tokens, cot, far_oth, own)
    first = core_swap(packed)
    others = core_swap(tokens)

    t0, t1 = gradients(tokens, first, cot, first, far, cuts=((0, half), (half, ROWS)))
    (t1,) = held_until((t1,), (others,))
    t0, t1 = y_up(t0), y_down(t1)
    p_11, p_1m, p_02, p_0m, p_01, p_10, p_00 = gradients(
        tokens, others, cot, first, rest
    )
    p_11 = p_11.at[:half].add(t0)
    p_1m = p_1m.at[half:].add(t1)
    p_11, p_1m, p_02 = held_until((p_11, p_1m, p_02), (w_0m, w_01, w_10))
    key_own, key_oth, grad_in, back = forward(
        tokens, others, cot, first, (w_0m, w_01, w_10, own), near, (p_11, p_1m, p_02)
    )
    p_11, p_1m, p_02 = y_up(p_11), z_across(p_1m), y_down(p_02)
    p_0m = (p_0m.astype(F32) + p_1m.astype(F32) + p_02.astype(F32)).astype(BF16)
    p_10 = (p_10.astype(F32) + p_11.astype(F32)).astype(BF16)
    grad_in = unpack(grad_in, core_swap(back), near_oth)
    (p_01,) = held_until((p_01,), (key_own,))
    (own,) = held_until((own,), (p_0m, p_10, grad_in))
    p_0m, p_01, p_10 = y_down(p_0m), y_up(p_01), z_across(p_10)
    partner_params = partner_swap(own, bit)
    gradient = (p_00.astype(F32) + p_01.astype(F32)) + (p_0m.astype(F32) + p_10.astype(F32))
    moved = 0.9 * momentum + gradient

    w_0m, w_10 = held_until((w_0m, w_10), (p_0m, p_01, p_10, partner_params))
    w_02, w_11, w_1m = y_up(w_0m), y_down(w_10), z_across(w_0m)
    partner_moved = partner_swap(moved.astype(BF16), bit)
    pieces = w_1m[:half], w_11[half:]
    halves = y_up(pieces[0]), y_down(pieces[1])
    theirs = partner_moved.astype(F32)
    new_momentum = 0.5 * (moved + theirs)
    partner_stepped = partner_params.astype(F32) - 0.1 * theirs
    new_params = 0.5 * ((params - 0.1 * moved) + partner_stepped)
    key_own, key_oth, grad_in, back = forward(
        tokens,
        others,
        cot,
        first,
        (w_11, w_1m, w_02),
        mid,
        (partner_moved, *pieces),
        (key_own, key_oth),
        grad_in,
    )
    key_oth = core_swap(key_oth)
    (w_12,) = held_until((jnp.concatenate(halves, axis=0),), (new_params, new_momentum))
    w_12_oth = core_swap(w_12)
    grad_in = unpack(grad_in, core_swap(back), mid_oth)
    key_own, grad_in = one_shard(tokens, cot, w_12, key_own, grad_in, far)
    key_out, grad_in = one_shard(tokens, cot, w_12_oth, key_own, grad_in, far_oth, key_oth)
    return key_out[None], grad_in[None], new_params[None], new_momentum[None]


def solution(mesh):
    rows = P("rep", "fsdp", None)
    return jax.shard_map(
        body,
        mesh=mesh,
        in_specs=(P(), rows, rows, rows, rows),
        out_specs=(rows, rows, rows, rows),
        check_vma=False,
    )
```

```python
import jax
import jax.numpy as jnp
from jax import lax
from jax.experimental import pallas as pl
from jax.experimental.pallas import tpu as pltpu
from jax.sharding import PartitionSpec as P

D = 8192
KV = 1024
ROWS = 512
NZ, NY, NC = 2, 4, 2
SCALE = D ** (-0.5)
LEVELS = 3
TN = (((0,), (0,)), ((), ()))
NT = (((1,), (1,)), ((), ()))
NN = (((1,), (0,)), ((), ()))
F32, BF16 = jnp.float32, jnp.bfloat16

FAR = ((1, 2),)
MIDDLE = ((1, 1), (1, -1), (0, 2))
NEAR = ((0, -1), (0, 1), (1, 0), (0, 0))


def place(z, y, c):
    return (z % NZ) * NY * NC + (y % NY) * NC + c % NC


def shift(dz=0, dy=0, dc=0):
    return [
        (place(z, y, c), place(z + dz, y + dy, c + dc))
        for z in range(NZ)
        for y in range(NY)
        for c in range(NC)
    ]


def y_up(value):
    return lax.ppermute(value, "fsdp", shift(dy=1))


def y_down(value):
    return lax.ppermute(value, "fsdp", shift(dy=-1))


def z_across(value):
    return lax.ppermute(value, "fsdp", shift(dz=1))


def core_swap(value):
    return lax.ppermute(value, "fsdp", shift(dc=1))


def partner_swap(value, bit):
    def swap(arr, level):
        return lax.ppermute(arr, "rep", [(r, r ^ (1 << level)) for r in range(1 << LEVELS)])

    return lax.switch(bit, [lambda arr, level=level: swap(arr, level) for level in range(LEVELS)], value)


def columns(offsets, core):
    f = lax.axis_index("fsdp").astype(jnp.int32)
    z, y = f // (NY * NC), (f // NC) % NY
    return jnp.stack([place(z + dz, y + dy, core).astype(jnp.int32) for dz, dy in offsets])


def dot(a, b, dims):
    return lax.dot_general(a, b, dims, preferred_element_type=F32)


def whole(shape):
    return pl.BlockSpec(shape, lambda k, idx: (0,) * len(shape))


def by_column():
    return pl.BlockSpec((ROWS, ROWS), lambda k, idx: (0, idx[k]))


def by_step():
    return pl.BlockSpec((1, ROWS, ROWS), lambda k, idx: (k, 0, 0))


def params_of(flops, nbytes, vmem=36):
    flops, nbytes = int(flops), int(nbytes)
    return dict(
        compiler_params=pltpu.CompilerParams(vmem_limit_bytes=vmem * 2**20),
        cost_estimate=pl.CostEstimate(flops=flops, bytes_accessed=nbytes, transcendentals=0),
    )


ANYWHERE = pl.BlockSpec(memory_space=pl.ANY)
IN_HBM = pl.BlockSpec(memory_space=pltpu.HBM)


def slab(idx_ref, k):
    return pl.ds(pl.multiple_of(idx_ref[k] * ROWS, ROWS), ROWS)


def token_slabs(idx_ref, tok_ref, buf, sem, n):
    step = pl.program_id(0)

    def copy(k):
        return pltpu.make_async_copy(tok_ref.at[:, slab(idx_ref, k)], buf.at[k], sem.at[k])

    @pl.when(step == 0)
    def _():
        for k in range(n):
            copy(k).start()

    for k in range(n):

        @pl.when(step == k)
        def _(k=k):
            copy(k).wait()

    return buf[step]


def slab_scratch(n):
    return [pltpu.VMEM((n, ROWS, ROWS), BF16), pltpu.SemaphoreType.DMA((n,))]


def through(in_copies, out_copies):
    for copy in in_copies:
        copy.start()
    for copy, out in zip(in_copies, out_copies):
        copy.wait()
        out.start()
    for out in out_copies:
        out.wait()


def pack_first(tokens, cot, idx, after):
    def kernel(idx_ref, tok_ref, cot_ref, after_ref, out_ref, buf, sem, out_sem):
        del after_ref
        n, rows = 4, ROWS // 4
        ins, outs = [], []
        for i in range(n):
            part = pl.ds(i * rows, rows)
            tok_part, tok_buf = tok_ref.at[part, slab(idx_ref, 0)], buf.at[part, pl.ds(KV, ROWS)]
            ins.append(pltpu.make_async_copy(cot_ref.at[part], buf.at[part, pl.ds(0, KV)], sem.at[i]))
            ins.append(pltpu.make_async_copy(tok_part, tok_buf, sem.at[n + i]))
            outs.append(pltpu.make_async_copy(buf.at[part], out_ref.at[part], out_sem.at[i]))
        for copy in ins:
            copy.start()
        for i in range(n):
            ins[2 * i].wait()
            ins[2 * i + 1].wait()
            outs[i].start()
        for copy in outs:
            copy.wait()

    shape = (ROWS, KV + ROWS)
    return pl.pallas_call(
        kernel,
        grid_spec=pltpu.PrefetchScalarGridSpec(
            num_scalar_prefetch=1,
            grid=(1,),
            in_specs=[IN_HBM, ANYWHERE, ANYWHERE],
            out_specs=ANYWHERE,
            scratch_shapes=[
                pltpu.VMEM(shape, BF16),
                pltpu.SemaphoreType.DMA((8,)),
                pltpu.SemaphoreType.DMA((4,)),
            ],
        ),
        out_shape=jax.ShapeDtypeStruct(shape, BF16),
        name="pack_first",
        **params_of(0, 3 * 2**20, 58),
    )(idx, tokens, cot, after)


def unpack(target, pieces, idx):
    n = idx.shape[0]

    def kernel(idx_ref, old_ref, piece_ref, out_ref, buf, sem, out_sem):
        del old_ref
        through(
            [pltpu.make_async_copy(piece_ref.at[k], buf.at[k], sem.at[k]) for k in range(n)],
            [
                pltpu.make_async_copy(buf.at[k], out_ref.at[:, slab(idx_ref, k)], out_sem.at[k])
                for k in range(n)
            ],
        )

    return pl.pallas_call(
        kernel,
        grid_spec=pltpu.PrefetchScalarGridSpec(
            num_scalar_prefetch=1,
            grid=(1,),
            in_specs=[ANYWHERE] * 2,
            out_specs=ANYWHERE,
            scratch_shapes=[
                pltpu.VMEM((n, ROWS, ROWS), BF16),
                pltpu.SemaphoreType.DMA((n,)),
                pltpu.SemaphoreType.DMA((n,)),
            ],
        ),
        out_shape=jax.ShapeDtypeStruct(target.shape, BF16),
        input_output_aliases={1: 0},
        name="unpack",
        **params_of(0, n * 2**20),
    )(idx, target, pieces)


def held_until(values, after):
    after = [array[:16, :128] if array.size > ROWS * KV or array.dtype == F32 else array for array in after]
    n, m = len(values), len(after)

    def kernel(*refs):
        del refs

    return pl.pallas_call(
        kernel,
        in_specs=[ANYWHERE] * (n + m),
        out_specs=[ANYWHERE] * n,
        out_shape=[jax.ShapeDtypeStruct(v.shape, v.dtype) for v in values],
        input_output_aliases={i: i for i in range(n)},
        name="held_until",
        **params_of(0, 0),
    )(*values, *after)


def gradients(tokens, other_tokens, cot, first, idx, cuts=None, after=()):
    n = idx.shape[0]
    if cuts is None:
        shapes = [(ROWS, KV)] * n
    else:
        shapes = [(hi - lo, KV) for lo, hi in cuts]

    def kernel(idx_ref, tok_ref, oth_ref, cot_ref, cot_oth_ref, *outs):
        outs = outs[len(after) :]
        outs, scratch = outs[: len(shapes)], outs[len(shapes) :]
        tok = token_slabs(idx_ref, tok_ref, *scratch[:2], n)
        step = pl.program_id(0)
        oth = oth_ref[...] if cuts is not None else token_slabs(idx_ref, oth_ref, *scratch[2:], n)
        total = dot(tok, cot_ref[...], TN) + dot(oth, cot_oth_ref[...], TN)
        total = (total * SCALE).astype(BF16)
        if cuts is not None:
            for (lo, hi), out in zip(cuts, outs):
                out[...] = total[lo:hi]
        else:
            for i, out in enumerate(outs):

                @pl.when(step == i)
                def _(out=out):
                    out[...] = total

    if cuts is not None:
        oth_spec = pl.BlockSpec((ROWS, ROWS), lambda k, idx: (0, KV // ROWS))
    else:
        oth_spec = IN_HBM
    return pl.pallas_call(
        kernel,
        grid_spec=pltpu.PrefetchScalarGridSpec(
            num_scalar_prefetch=1,
            grid=(n,),
            in_specs=[IN_HBM, oth_spec, whole((ROWS, KV)), whole((ROWS, KV))]
            + [ANYWHERE] * len(after),
            out_specs=[whole(s) for s in shapes],
            scratch_shapes=slab_scratch(n) * (1 if cuts is not None else 2),
        ),
        out_shape=[jax.ShapeDtypeStruct(s, BF16) for s in shapes],
        name="gradients",
        **params_of(n * 4 * ROWS * ROWS * KV, (2 * n + 2) * 2**20, 58 if n == 1 else 36),
    )(idx, tokens, other_tokens, cot, first, *after)


def forward(tokens, other_tokens, cot, first, weights, idx, after, keys=None, grad_in=None):
    n, m = idx.shape[0], len(after)
    last = keys is not None

    def kernel(idx_ref, tok_ref, oth_ref, cot_ref, cot_oth_ref, *refs):
        w_refs, rest = refs[:n], refs[n + m :]
        if last:
            own_in, oth_in, _, own_out, oth_out, gi_ref, back_ref, *rest, acc = rest
        else:
            own_out, oth_out, gi_ref, back_ref, *rest = rest
            acc = oth_out
        w_buf, sem, *slabs = rest
        step = pl.program_id(0)

        @pl.when(step == 0)
        def _():
            for i, w_ref in enumerate(w_refs):
                pltpu.make_async_copy(w_ref, w_buf.at[i], sem.at[i]).start()
            if last:
                own_out[...] = own_in[...]
                acc[...] = oth_in[...]
            else:
                own_out[...] = jnp.zeros_like(own_out)
                acc[...] = jnp.zeros_like(acc)

        for i, w_ref in enumerate(w_refs):

            @pl.when(step == i)
            def _(i=i, w_ref=w_ref):
                pltpu.make_async_copy(w_ref, w_buf.at[i], sem.at[i]).wait()

        w = w_buf[step]
        tok = token_slabs(idx_ref, tok_ref, *slabs[:2], n)
        oth = token_slabs(idx_ref, oth_ref, *slabs[2:], n)
        own_out[...] += dot(tok, w, NN)
        acc[...] += dot(oth, w, NN)
        gi_ref[...] = (dot(cot_ref[...], w, NT) * SCALE).astype(BF16)
        back_ref[0] = (dot(cot_oth_ref[...], w, NT) * SCALE).astype(BF16)

        if last:

            @pl.when(step == n - 1)
            def _():
                oth_out[...] = (acc[...] * SCALE).astype(BF16)

    in_specs = [IN_HBM, IN_HBM, whole((ROWS, KV)), whole((ROWS, KV))]
    in_specs += [ANYWHERE] * (n + m)
    operands = [tokens, other_tokens, cot, first, *weights, *after]
    aliases = {}
    scratch = [pltpu.VMEM((n, ROWS, KV), BF16), pltpu.SemaphoreType.DMA((n,)), *slab_scratch(n) * 2]
    if last:
        in_specs += [whole((ROWS, KV))] * 2 + [ANYWHERE]
        operands += [*keys, grad_in]
        aliases = {len(operands): 2}
        scratch += [pltpu.VMEM((ROWS, KV), F32)]
    return pl.pallas_call(
        kernel,
        grid_spec=pltpu.PrefetchScalarGridSpec(
            num_scalar_prefetch=1,
            grid=(n,),
            in_specs=in_specs,
            out_specs=[whole((ROWS, KV)), whole((ROWS, KV)), by_column(), by_step()],
            scratch_shapes=scratch,
        ),
        out_shape=[
            jax.ShapeDtypeStruct((ROWS, KV), F32),
            jax.ShapeDtypeStruct((ROWS, KV), BF16 if last else F32),
            jax.ShapeDtypeStruct((ROWS, D), BF16),
            jax.ShapeDtypeStruct((n, ROWS, ROWS), BF16),
        ],
        input_output_aliases=aliases,
        name="forward",
        **params_of(n * 8 * ROWS * ROWS * KV, (3 * n + 8) * 2**20),
    )(idx, *operands)


def one_shard(tokens, cot, weights, keys, grad_in, idx, received=None):
    final = received is not None
    tile = ROWS // 2

    def kernel(idx_ref, tok_ref, cot_ref, w_ref, key_ref, *rest):
        *rest, tok_buf, sem = rest
        step, n = pl.program_id(0), ROWS // tile
        part = [pl.ds(i * tile, tile) for i in range(n)]
        copies = [
            pltpu.make_async_copy(tok_ref.at[p, slab(idx_ref, 0)], tok_buf.at[p], sem.at[i])
            for i, p in enumerate(part)
        ]

        @pl.when(step == 0)
        def _():
            for copy in copies:
                copy.start()

        for i, copy in enumerate(copies):

            @pl.when(step == i)
            def _(copy=copy):
                copy.wait()

        tok = tok_buf[pl.ds(pl.multiple_of(step * tile, tile), tile)]
        total = key_ref[...] + dot(tok, w_ref[...], NN)
        if final:
            rec_ref, _, key_out, gi_ref = rest
            key_out[...] = (total * SCALE + rec_ref[...].astype(F32)).astype(BF16)
        else:
            _, key_out, gi_ref = rest
            key_out[...] = total
        gi_ref[...] = (dot(cot_ref[...], w_ref[...], NT) * SCALE).astype(BF16)

    def wide():
        return pl.BlockSpec((tile, KV), lambda k, idx: (k, 0))

    def narrow():
        return pl.BlockSpec((tile, ROWS), lambda k, idx: (k, idx[0]))

    operands = [tokens, cot, weights, keys] + ([received] if final else []) + [grad_in]
    return pl.pallas_call(
        kernel,
        grid_spec=pltpu.PrefetchScalarGridSpec(
            num_scalar_prefetch=1,
            grid=(ROWS // tile,),
            in_specs=[IN_HBM, wide(), whole((ROWS, KV)), wide()]
            + ([wide()] if final else [])
            + [ANYWHERE],
            out_specs=[wide(), narrow()],
            scratch_shapes=[
                pltpu.VMEM((ROWS, ROWS), BF16),
                pltpu.SemaphoreType.DMA((ROWS // tile,)),
            ],
        ),
        out_shape=[
            jax.ShapeDtypeStruct((ROWS, KV), BF16 if final else F32),
            jax.ShapeDtypeStruct((ROWS, D), BF16),
        ],
        input_output_aliases={len(operands): 1},
        name="one_shard",
        **params_of(4 * ROWS * ROWS * KV, 8 * 2**20, 36 if final else 57),
    )(idx, *operands)


def body(round_index, tokens, cotangent, params, momentum):
    tokens, cot, params, momentum = tokens[0], cotangent[0], params[0], momentum[0]
    bit = jnp.mod(round_index, LEVELS)
    half = ROWS // 2
    core = lax.axis_index("fsdp").astype(jnp.int32) % NC
    far, far_oth = columns(FAR, core), columns(FAR, 1 - core)
    mid, mid_oth = columns(MIDDLE, core), columns(MIDDLE, 1 - core)
    near, near_oth = columns(NEAR, core), columns(NEAR, 1 - core)
    rest = columns(MIDDLE + NEAR, core)

    own = params.astype(BF16)
    w_0m, w_01, w_10 = y_up(own), y_down(own), z_across(own)

    packed = pack_first(tokens, cot, far_oth, own)
    first = core_swap(packed)
    others = core_swap(tokens)

    t0, t1 = gradients(tokens, first, cot, first, far, cuts=((0, half), (half, ROWS)))
    (t1,) = held_until((t1,), (others,))
    t0, t1 = y_up(t0), y_down(t1)
    p_11, p_1m, p_02, p_0m, p_01, p_10, p_00 = gradients(
        tokens, others, cot, first, rest
    )
    p_11 = p_11.at[:half].add(t0)
    p_1m = p_1m.at[half:].add(t1)
    p_11, p_1m, p_02 = held_until((p_11, p_1m, p_02), (w_0m, w_01, w_10))
    key_own, key_oth, grad_in, back = forward(
        tokens, others, cot, first, (w_0m, w_01, w_10, own), near, (p_11, p_1m, p_02)
    )
    p_11, p_1m, p_02 = y_up(p_11), z_across(p_1m), y_down(p_02)
    p_0m = (p_0m.astype(F32) + p_1m.astype(F32) + p_02.astype(F32)).astype(BF16)
    p_10 = (p_10.astype(F32) + p_11.astype(F32)).astype(BF16)
    grad_in = unpack(grad_in, core_swap(back), near_oth)
    (p_01,) = held_until((p_01,), (key_own,))
    (own,) = held_until((own,), (p_0m, p_10, grad_in))
    p_0m, p_01, p_10 = y_down(p_0m), y_up(p_01), z_across(p_10)
    partner_params = partner_swap(own, bit)
    gradient = (p_00.astype(F32) + p_01.astype(F32)) + (p_0m.astype(F32) + p_10.astype(F32))
    moved = 0.9 * momentum + gradient

    w_0m, w_10 = held_until((w_0m, w_10), (p_0m, p_01, p_10, partner_params))
    w_02, w_11, w_1m = y_up(w_0m), y_down(w_10), z_across(w_0m)
    partner_moved = partner_swap(moved.astype(BF16), bit)
    pieces = w_1m[:half], w_11[half:]
    halves = y_up(pieces[0]), y_down(pieces[1])
    theirs = partner_moved.astype(F32)
    new_momentum = 0.5 * (moved + theirs)
    partner_stepped = partner_params.astype(F32) - 0.1 * theirs
    new_params = 0.5 * ((params - 0.1 * moved) + partner_stepped)
    key_own, key_oth, grad_in, back = forward(
        tokens,
        others,
        cot,
        first,
        (w_11, w_1m, w_02),
        mid,
        (partner_moved, *pieces),
        (key_own, key_oth),
        grad_in,
    )
    key_oth = core_swap(key_oth)
    (w_12,) = held_until((jnp.concatenate(halves, axis=0),), (new_params, new_momentum))
    w_12_oth = core_swap(w_12)
    grad_in = unpack(grad_in, core_swap(back), mid_oth)
    key_own, grad_in = one_shard(tokens, cot, w_12, key_own, grad_in, far)
    key_out, grad_in = one_shard(tokens, cot, w_12_oth, key_own, grad_in, far_oth, key_oth)
    return key_out[None], grad_in[None], new_params[None], new_momentum[None]


def solution(mesh):
    rows = P("rep", "fsdp", None)
    return jax.shard_map(
        body,
        mesh=mesh,
        in_specs=(P(), rows, rows, rows, rows),
        out_specs=(rows, rows, rows, rows),
        check_vma=False,
    )
```
